32 devices in a mesh: param: 4 (over y, x), space: 2 (over core), term: 4 (over z).
Axes of the slice: x: 2, y: 2, z: 4, core: 2. Of those that a mesh axis runs over, the one named last changes fastest.
Arguments:
- fields: float32 [16, 2, 8, 128, 128], P('param', None, None, 'space'), may hold values from -4 to 4
- library: int32 [168, 4], P('term'), may hold values from 0 to 6, as said below
- centers_x: int32 [16], replicated, may hold values from 0 to 127
- centers_y: int32 [16], replicated, may hold values from 0 to 127
- centers_t: int32 [4], replicated, may hold values from 0 to 7
- groups: int32 [168], replicated, may hold values from 0 to 23
Outputs:
- coefficients: float32 [16, 2, 168], P(('param', 'term'))
- misfit: float32 [16, 2, 168], P(('param', 'term'))
The draws below stay inside these ranges and needn't reach their ends.
Inputs may be any that keep to these rules, and one draw needn't show every extreme that they name: `library`: each row (a, b, dx, dy) gives powers a and b of 0 to 6 and derivative orders dx and dy of 0 to 2; rows are distinct, and a = b = 0 only with dx = dy = 0.
All inputs are finite; a program needn't handle non-finite values.
Results may differ from the reference program's by a relative error of at most 0.00011.
Values sent between devices are 32-bit elements; how exact they have to be, the bound alone decides.
No kernel may reach another device: no remote copies, remote signals or barrier semaphores. Data moves between devices by JAX's collectives and lax.ppermute only.
A program may use at most 64 MiB of HBM per device.

```python
import jax
import jax.numpy as jnp
from jax import lax

NX = 128
NY = 128
NT = 8
POWERS = 7
TERMS = 168
KX = 16
KY = 16
KT = 4
TESTS = 1024
RX = 16
RT = 4
GROUPS = 24
PARAMS = 16


def draw_library(key, part):
    combos = POWERS * POWERS * 9 - 8
    chosen = jax.random.permutation(key, combos)[:TERMS].astype(jnp.int32)
    code_value = jnp.where(chosen == 0, 0, chosen + 8).astype(jnp.int32)
    return jnp.stack([code_value // (9 * POWERS), code_value // 9 % POWERS, code_value % 9 // 3, code_value % 3], axis=1).astype(jnp.int32)


def set_ends(values, stream_key, least, high):
    longest = values.shape.index(max(values.shape))
    spots = []
    for shift in (0, 1):
        where = [jax.random.randint(jax.random.fold_in(stream_key, axis), (), 0, length) for axis, length in enumerate(values.shape)]
        where[longest] = (where[longest] + shift) % values.shape[longest]
        spots.append(tuple(where))
    return values.at[spots[0]].set(least).at[spots[1]].set(high)


def levels(own_key, dims, split, smallest, top_value):
    loudness = 1.0
    for position, shards_of in split:
        heights = jax.random.uniform(jax.random.fold_in(jax.random.fold_in(own_key, 6), position), (shards_of,), jnp.float32, smallest / len(split), top_value / len(split))
        loudness = loudness * jnp.repeat(jnp.exp(heights), dims[position] // shards_of).reshape((-1,) + (1,) * (len(dims) - 1 - position))
    return loudness


def noise(own_key, dims, spread, reach, cuts=(), kind=jnp.bfloat16):
    factor_of = levels(own_key, dims, cuts, -0.22, 0.18) if cuts else 1.0
    result = jax.random.normal(own_key, dims, jnp.float32) * spread * factor_of
    return jnp.minimum(jnp.maximum(result, -reach), reach).astype(kind)


def setup_inputs(seed: int = 0) -> dict:
    keys = jax.random.split(jax.random.key(seed), 7)
    return {
        "fields": noise(keys[0], (PARAMS, 2, NT, NX, NY), 0.8, 4.0, ((0, 4), (3, 2)), jnp.float32),
        "library": draw_library(jax.random.fold_in(keys[6], 71), 0),
        "centers_x": set_ends(jax.random.randint(keys[2], (KX,), 0, NX), jax.random.fold_in(keys[2], 1), 0, NX - 1).astype(jnp.int32),
        "centers_y": set_ends(jax.random.randint(keys[3], (KY,), 0, NY), jax.random.fold_in(keys[3], 1), 0, NY - 1).astype(jnp.int32),
        "centers_t": set_ends(jax.random.randint(keys[4], (KT,), 0, NT), jax.random.fold_in(keys[4], 1), 0, NT - 1).astype(jnp.int32),
        "groups": set_ends(jax.random.randint(keys[5], (TERMS,), 0, GROUPS), jax.random.fold_in(keys[5], 1), 0, GROUPS - 1).astype(jnp.int32),
    }


highest = lax.Precision.HIGHEST

def space_table(centers, first_row, row_count, extent):
    cell_index = first_row + jnp.arange(row_count, dtype=jnp.int32)
    offset = (cell_index[None, :] - centers[:, None] + extent // 2) % extent - extent // 2
    scaled = offset.astype(jnp.float32) / RX
    bump_base = 1.0 - scaled * scaled
    inside = jnp.abs(scaled) < 1.0
    cube = bump_base * bump_base * bump_base
    bump_value = jnp.where(inside, cube * bump_base, 0.0)
    bump_first = jnp.where(inside, 8.0 * scaled * cube / RX, 0.0)
    bump_second = jnp.where(inside, -8.0 * (cube - 6.0 * scaled * scaled * bump_base * bump_base) / (RX * RX), 0.0)
    return jnp.stack([bump_value, bump_first, bump_second]).astype(jnp.float32)

def time_table(centers):
    step_index = jnp.arange(NT, dtype=jnp.int32)
    scaled = (step_index[None, :] - centers[:, None]).astype(jnp.float32) / RT
    bump_base = 1.0 - scaled * scaled
    inside = jnp.abs(scaled) < 1.0
    time_bump = jnp.where(inside, bump_base * bump_base, 0.0).astype(jnp.float32)
    time_slope = jnp.where(inside, 4.0 * scaled * bump_base / RT, 0.0).astype(jnp.float32)
    return (time_bump, time_slope)

def term_codes(library):
    return ((library[:, 0] * POWERS + library[:, 1]) * 9 + library[:, 2] * 3 + library[:, 3]).astype(jnp.int32)

def weak_rows(field_pair, x_table, y_table, time_bump, time_slope, term_code):
    species_u = field_pair[0]
    species_v = field_pair[1]
    powers_u = [jnp.ones_like(species_u)]
    powers_v = [jnp.ones_like(species_v)]
    for degree in range(1, POWERS):
        powers_u.append(powers_u[-1] * species_u)
        powers_v.append(powers_v[-1] * species_v)
    stack_u = jnp.stack(powers_u)
    stack_v = jnp.stack(powers_v)
    monomials = (stack_u[:, None] * stack_v[None, :]).reshape((POWERS * POWERS,) + species_u.shape)
    across_y = jnp.einsum('mtxy,dky->mtxdk', monomials, y_table, precision=highest)
    across_t = jnp.einsum('mtxdk,rt->mrxdk', across_y, time_bump, precision=highest)
    across_x = jnp.einsum('mrxdk,elx->medrkl', across_t, x_table, precision=highest)
    flat_table = across_x.reshape(POWERS * POWERS * 9, KT * KY * KX)
    features = jnp.take(flat_table, term_code, axis=0)
    source = across_y[jnp.array([POWERS, 1], dtype=jnp.int32)][:, :, :, 0, :]
    targets = jnp.einsum('stxk,rt,lx->srkl', source, time_slope, x_table[0], precision=highest)
    return jnp.concatenate([features, targets.reshape(2, KT * KY * KX)], axis=0)

def normalize(gram_matrix):
    diagonal = jnp.diagonal(gram_matrix, axis1=1, axis2=2)
    row_scale = jnp.sqrt(diagonal / TESTS + 1e-06)
    term_scale = row_scale[:, :TERMS]
    correlation = gram_matrix[:, :TERMS, :TERMS] / (TESTS * term_scale[:, :, None] * term_scale[:, None, :])
    right_side = gram_matrix[:, TERMS:, :TERMS] / (TESTS * term_scale[:, None, :] * row_scale[:, TERMS:, None])
    frobenius = jnp.sqrt(lax.optimization_barrier(jnp.sum(correlation * correlation, axis=(1, 2))))
    return (correlation, right_side, frobenius)

def group_squares(values, onehot):
    return jnp.dot(lax.optimization_barrier(jnp.sum(values * values, axis=(0, 1))), onehot, precision=highest)

def shrink(values, totals, onehot):
    threshold = 0.7 * jnp.sqrt(jnp.mean(totals))
    per_term = jnp.dot(onehot, totals, precision=highest)
    factor = jnp.maximum(0.0, 1.0 - threshold / jnp.sqrt(per_term + 1e-12))
    return values * factor

def correlate(correlation, values):
    return jnp.einsum('pij,psj->psi', correlation, values, precision=highest)

def reference(fields, library, centers_x, centers_y, centers_t, groups):
    x_table = space_table(centers_x, 0, NX, NX)
    y_table = space_table(centers_y, 0, NY, NY)
    time_bump, time_slope = time_table(centers_t)
    term_code = term_codes(library)

    def one_param(field_pair):
        integrals = weak_rows(field_pair, x_table, y_table, time_bump, time_slope, term_code)
        return jnp.dot(integrals, integrals.T, precision=highest)
    gram_matrix = lax.map(one_param, fields)
    correlation, right_side, frobenius = normalize(gram_matrix)
    onehot = (groups[:, None] == jnp.arange(GROUPS, dtype=jnp.int32)[None, :]).astype(jnp.float32)
    step_size = 1.0 / jnp.max(frobenius)
    first_guess = step_size * right_side
    first = shrink(first_guess, group_squares(first_guess, onehot), onehot)
    second_guess = first - step_size * (correlate(correlation, first) - right_side)
    second = shrink(second_guess, group_squares(second_guess, onehot), onehot)
    coefficients = second / step_size
    misfit = right_side - correlate(correlation, second)
    return (coefficients, misfit)
```

```python
import functools

import jax
import jax.numpy as jnp
from jax import lax
from jax.experimental import pallas as pl
from jax.experimental.pallas import tpu as pltpu
from jax.sharding import PartitionSpec as P

NX = 128
NY = 128
NT = 8
POWERS = 7
TERMS = 168
TESTS = 1024
KX = 16
KY = 16
KT = 4
RX = 16
RT = 4
GROUPS = 24
ROWS = 3 * KY
LANES = 4 * KT * KX
VMEM_LIMIT = 40 * 2**20

f32, bf16 = jnp.float32, jnp.bfloat16
NT_DIMS = ((1,), (1,))
NN_DIMS = ((1,), (0,))


def split(x):
    high = x.astype(bf16)
    return high, (x - high.astype(f32)).astype(bf16)


def dot(a, b, dims):
    return lax.dot_general(a, b, (dims, ((), ())), preferred_element_type=f32)


def dot3(a, b, dims):
    ah, al = split(a)
    bh, bl = split(b)
    return dot(ah, bh, dims) + (dot(ah, bl, dims) + dot(al, bh, dims))


def space_rows(offset):
    scaled = offset.astype(f32) * (1.0 / RX)
    base = 1.0 - scaled * scaled
    inside = jnp.abs(scaled) < 1.0
    cube = base * base * base
    value = jnp.where(inside, cube * base, 0.0)
    first = jnp.where(inside, 8.0 * scaled * cube * (1.0 / RX), 0.0)
    second = jnp.where(
        inside, -8.0 * (cube - 6.0 * scaled * scaled * base * base) * (1.0 / (RX * RX)), 0.0
    )
    return value, first, second


def integrals_kernel(
    rows, where, cx, cy, ct, fields, out, pair, power_u, powers_v, y_split, tx_split, high, low, sem
):
    cells = NT * rows
    copy = pltpu.make_async_copy(fields.at[where[0]], pair, sem)
    copy.start()
    row = lax.broadcasted_iota(jnp.int32, (KY, NY), 0)
    lane = lax.broadcasted_iota(jnp.int32, (KY, NY), 1)
    center = jnp.zeros((KY, NY), jnp.int32)
    for k in range(KY):
        center = jnp.where(row == k, cy[k], center)
    offset = ((lane - center + NY // 2) & (NY - 1)) - NY // 2
    for i, part in enumerate(split(jnp.concatenate(space_rows(offset), axis=0))):
        y_split[pl.ds(i * ROWS, ROWS), :] = jnp.concatenate([part, part], axis=1)
    lane = lax.broadcasted_iota(jnp.int32, (1, LANES), 1)
    slot, kt, kx = lane >> 6, (lane >> 4) & 3, lane & 15
    center_x = jnp.zeros((1, LANES), jnp.int32)
    center_t = jnp.zeros((1, LANES), jnp.int32)
    for k in range(KX):
        center_x = jnp.where(kx == k, cx[k], center_x)
    for k in range(KT):
        center_t = jnp.where(kt == k, ct[k], center_t)
    row = lax.broadcasted_iota(jnp.int32, (rows, LANES), 0) + where[1]
    offset = ((row - center_x + NX // 2) & (NX - 1)) - NX // 2
    value, first, second = space_rows(offset)
    x_table = jnp.where(slot == 1, first, jnp.where(slot == 2, second, value))
    for t in range(NT):
        scaled = (t - center_t).astype(f32) * (1.0 / RT)
        base = 1.0 - scaled * scaled
        weight = jnp.where(slot == 3, 4.0 * scaled * base * (1.0 / RT), base * base)
        weight = jnp.where(jnp.abs(scaled) < 1.0, weight, 0.0)
        for i, part in enumerate(split(x_table * weight)):
            tx_split[i, pl.ds(t * rows, rows), :] = part
    copy.wait()
    power_u[...] = jnp.ones((cells, NY), f32)
    v = pair[1].reshape(cells, NY)
    power = v
    powers_v[0] = v
    for b in range(1, POWERS - 1):
        power = power * v
        powers_v[b] = power
    tile = 256

    def one_power(a, _):
        for b in range(POWERS):
            for h in range(cells // tile):
                part = pl.ds(h * tile, tile)
                monomial = power_u[part, :]
                if b:
                    monomial = monomial * powers_v[b - 1, part, :]
                both = jnp.concatenate(split(monomial), axis=1)
                across = dot(y_split[...], both, NT_DIMS)
                across_high, across_low = split(across[:ROWS] + across[ROWS:])
                high[pl.ds(b * ROWS, ROWS), part] = across_high
                low[pl.ds(b * ROWS, ROWS), part] = across_low
        result = (
            dot(high[...], tx_split[0], NN_DIMS)
            + dot(low[...], tx_split[0], NN_DIMS)
            + dot(high[...], tx_split[1], NN_DIMS)
        )
        span = POWERS * ROWS
        place = pl.ds(pl.multiple_of(a * span, 8), span)
        out[0, place, :] = result[:, :128]
        out[1, place, :] = result[:, 128:]
        power_u[...] = power_u[...] * pair[0].reshape(cells, NY)
        return 0

    lax.fori_loop(0, POWERS, one_power, 0)


def integrals(where, cx, cy, ct, fields):
    rows = fields.shape[3]
    cells = NT * rows
    smem = pl.BlockSpec(memory_space=pltpu.SMEM)
    return pl.pallas_call(
        functools.partial(integrals_kernel, rows),
        out_shape=jax.ShapeDtypeStruct((2, POWERS * POWERS * ROWS, 128), f32),
        in_specs=[smem] * 4 + [pl.BlockSpec(memory_space=pl.ANY)],
        out_specs=pl.BlockSpec(memory_space=pltpu.VMEM),
        scratch_shapes=[
            pltpu.VMEM((2, NT, rows, NY), f32),
            pltpu.VMEM((cells, NY), f32),
            pltpu.VMEM((POWERS - 1, cells, NY), f32),
            pltpu.VMEM((2 * ROWS, 2 * NY), bf16),
            pltpu.VMEM((2, cells, LANES), bf16),
            pltpu.VMEM((POWERS * ROWS, cells), bf16),
            pltpu.VMEM((POWERS * ROWS, cells), bf16),
            pltpu.SemaphoreType.DMA,
        ],
        compiler_params=pltpu.CompilerParams(vmem_limit_bytes=VMEM_LIMIT),
        cost_estimate=pl.CostEstimate(flops=10**10, bytes_accessed=3 * 10**6, transcendentals=0),
        name="integrals",
    )(where, cx, cy, ct, fields)


def pick_kernel(local, shares, me, *refs):
    libs = refs[:shares]
    flat, out = refs[shares:]
    lane = lax.broadcasted_iota(jnp.int32, (8, 128), 1)
    left = lane < 64

    def place(j, a, b, dx, dy):
        row = pl.multiple_of((a * POWERS + b) * ROWS + dy * KY, 8)
        chunk = dx >> 1
        odd = (dx & 1) == 1
        top = flat[chunk, pl.ds(row, 8), :]
        low = flat[chunk, pl.ds(row + 8, 8), :]
        even_value = jnp.where(left, top, pltpu.roll(low, 64, 1))
        odd_value = jnp.where(left, pltpu.roll(top, 64, 1), low)
        out[pl.ds(pl.multiple_of(j * 8, 8), 8), :] = jnp.where(odd, odd_value, even_value)

    for k in range(shares):
        owner = lax.rem(me[0] + k, shares)
        lib = libs[k]

        def term(i, _):
            place(owner * local + i, lib[i, 0], lib[i, 1], lib[i, 2], lib[i, 3])
            return 0

        lax.fori_loop(0, local, term, 0)
    place(TERMS, 1, 0, 3, 0)
    place(TERMS + 1, 0, 1, 3, 0)
    out[pl.ds((TERMS + 2) * 8, 48), :] = jnp.zeros((48, 128), f32)


def pick(where, libs, flat):
    shares = len(libs)
    smem = pl.BlockSpec(memory_space=pltpu.SMEM)
    vmem = pl.BlockSpec(memory_space=pltpu.VMEM)
    return pl.pallas_call(
        functools.partial(pick_kernel, libs[0].shape[0], shares),
        out_shape=jax.ShapeDtypeStruct(((TERMS + 8) * 8, 128), f32),
        in_specs=[smem] * (1 + shares) + [vmem],
        out_specs=vmem,
        compiler_params=pltpu.CompilerParams(vmem_limit_bytes=VMEM_LIMIT),
        name="pick",
    )(where, *libs, flat)


def fit_kernel(own, other, grp, payload, normal, dmat):
    pad = TERMS + 8
    gram = jnp.zeros((pad, pad), f32)
    for q in range(4):
        parts = []
        for s in (2 * q, 2 * q + 1):
            rows = pl.ds(s, pad, stride=8)
            parts.append(own[rows, :] + other[rows, :])
        x = jnp.concatenate(parts, axis=1)
        gram = gram + dot3(x, x, NT_DIMS)
    ri = lax.broadcasted_iota(jnp.int32, (pad, pad), 0)
    ci = lax.broadcasted_iota(jnp.int32, (pad, pad), 1)
    diagonal = jnp.where(ri == ci, gram, 0.0)
    dcol = jnp.sum(diagonal, axis=1, keepdims=True)
    drow = jnp.sum(diagonal, axis=0, keepdims=True)
    icol = 1.0 / jnp.sqrt(dcol * (1.0 / TESTS) + 1e-06)
    irow = 1.0 / jnp.sqrt(drow * (1.0 / TESTS) + 1e-06)
    norm = (gram * (icol * (1.0 / TESTS))) * irow
    norm = jnp.where(ci < TERMS, norm, 0.0)
    corr = norm[:TERMS, :TERMS]
    squares = jnp.sum(jnp.sum(corr * corr, axis=0, keepdims=True), axis=1, keepdims=True)
    normal[...] = norm[:, :TERMS]
    gi = lax.broadcasted_iota(jnp.int32, (GROUPS, TERMS), 0)
    onehot = gi == grp[...]
    quad = jnp.zeros((32, GROUPS * GROUPS + GROUPS), f32)
    for s in range(2):
        right = norm[TERMS + s : TERMS + s + 1, :TERMS]
        spread = jnp.where(onehot, right, 0.0)
        d = dot3(spread, corr, NN_DIMS)
        dmat[pl.ds(s * GROUPS, GROUPS), :] = d
        masked = [jnp.where(grp[...] == h, d, 0.0) for h in range(GROUPS)]
        masked = jnp.concatenate(masked + [spread], axis=0)
        left = jnp.concatenate([d, right, jnp.zeros((7, TERMS), f32)], axis=0)
        quad = quad + dot3(left, masked, NT_DIMS)
    width = payload.shape[1]
    payload[...] = jnp.zeros((32, width), f32)
    payload[:, : quad.shape[1]] = quad
    payload[pl.ds(31, 1), :] = jnp.broadcast_to(squares, (1, width))


def fit(own, other, grp):
    vmem = pl.BlockSpec(memory_space=pltpu.VMEM)
    return pl.pallas_call(
        fit_kernel,
        out_shape=(
            jax.ShapeDtypeStruct((32, 640), f32),
            jax.ShapeDtypeStruct((TERMS + 8, TERMS), f32),
            jax.ShapeDtypeStruct((2 * GROUPS, TERMS), f32),
        ),
        in_specs=[vmem] * 3,
        out_specs=(vmem,) * 3,
        compiler_params=pltpu.CompilerParams(vmem_limit_bytes=VMEM_LIMIT),
        name="fit",
    )(own, other, grp)


def column(row, n):
    ri = lax.broadcasted_iota(jnp.int32, (n, n), 0)
    ci = lax.broadcasted_iota(jnp.int32, (n, n), 1)
    return jnp.sum(jnp.where(ri == ci, row, 0.0), axis=1, keepdims=True)


def end_kernel(shares, grp, normal, dmat, *refs):
    pieces = refs[:shares]
    coef, misfit = refs[shares:]
    total = pieces[0][...]
    largest = total[31:32, :1]
    for piece in pieces[1:]:
        value = piece[...]
        total = total + value
        largest = jnp.maximum(largest, value[31:32, :1])
    step = 1.0 / jnp.sqrt(largest)
    wide = GROUPS * GROUPS
    quad = total[:GROUPS, :wide]
    cross = total[GROUPS : GROUPS + 1, :wide]
    rr = total[GROUPS : GROUPS + 1, wide : wide + GROUPS]

    def factor(totals):
        threshold = 0.7 * jnp.sqrt(jnp.sum(totals, axis=1, keepdims=True) * (1.0 / GROUPS))
        return jnp.maximum(0.0, 1.0 - threshold / jnp.sqrt(totals + 1e-12))

    f_row = factor(step * step * rr)
    f_col = column(f_row, GROUPS)
    ci = lax.broadcasted_iota(jnp.int32, (GROUPS, wide), 1)
    gi = lax.broadcasted_iota(jnp.int32, (GROUPS, wide), 0)
    block = (ci >= gi * GROUPS) & (ci < gi * GROUPS + GROUPS)
    first_col = jnp.sum(jnp.where(block, gi * GROUPS, 0), axis=0, keepdims=True)
    tiled = jnp.sum(jnp.where(ci - first_col == gi, f_col, 0.0), axis=0, keepdims=True)
    dd = jnp.sum(quad * f_col, axis=0, keepdims=True) * tiled
    rd = cross * tiled
    dd_col = jnp.sum(jnp.where(block, dd, 0.0), axis=1, keepdims=True)
    rd_col = jnp.sum(jnp.where(block, rd, 0.0), axis=1, keepdims=True)
    grow = 1.0 + f_col
    rr_col = column(rr, GROUPS)
    two_col = (step * step) * (grow * grow * rr_col - 2.0 * step * grow * rd_col + step * step * dd_col)
    two_col = jnp.maximum(two_col, 0.0)
    threshold = 0.7 * jnp.sqrt(jnp.sum(two_col, axis=0, keepdims=True) * (1.0 / GROUPS))
    f2_col = jnp.maximum(0.0, 1.0 - threshold / jnp.sqrt(two_col + 1e-12))
    g2 = lax.broadcasted_iota(jnp.int32, (GROUPS, TERMS), 0)
    onehot = g2 == grp[...]
    f_term = jnp.sum(jnp.where(onehot, f_col, 0.0), axis=0, keepdims=True)
    f2_term = jnp.sum(jnp.where(onehot, f2_col, 0.0), axis=0, keepdims=True)
    seconds = []
    for s in range(2):
        right = normal[pl.ds(TERMS + s, 1), :]
        pulled = jnp.sum(dmat[pl.ds(s * GROUPS, GROUPS), :] * f_col, axis=0, keepdims=True)
        seconds.append(step * ((1.0 + f_term) * right - step * pulled) * f2_term)
    second = jnp.concatenate(seconds + [jnp.zeros((6, TERMS), f32)], axis=0)
    coef[0] = (second / step)[:2]
    moved = dot3(second, normal[pl.ds(0, TERMS), :], NN_DIMS)
    misfit[0] = normal[pl.ds(TERMS, 2), :] - moved[:2]


def end(grp, normal, dmat, pieces):
    vmem = pl.BlockSpec(memory_space=pltpu.VMEM)
    shape = jax.ShapeDtypeStruct((1, 2, TERMS), f32)
    return pl.pallas_call(
        functools.partial(end_kernel, len(pieces)),
        out_shape=(shape, shape),
        in_specs=[vmem] * (3 + len(pieces)),
        out_specs=(vmem, vmem),
        compiler_params=pltpu.CompilerParams(vmem_limit_bytes=VMEM_LIMIT),
        name="finish",
    )(grp, normal, dmat, *pieces)


def body(fields, library, centers_x, centers_y, centers_t, groups):
    pgroup, rows = fields.shape[0], fields.shape[3]
    shares = lax.axis_size("term")
    local = library.shape[0]
    if pgroup != shares or local * shares != TERMS:
        raise ValueError("unexpected split")
    me = lax.axis_index("term")
    libs = [library]
    for k in range(1, shares):
        libs.append(lax.ppermute(library, "term", [((i + k) % shares, i) for i in range(shares)]))
    where = jnp.stack([me, lax.axis_index("space") * rows]).astype(jnp.int32)
    flat = integrals(where, centers_x, centers_y, centers_t, fields)
    own = pick(where, libs, flat)
    spaces = lax.axis_size("space")
    others = [
        lax.ppermute(own, "space", [((i + k) % spaces, i) for i in range(spaces)])
        for k in range(1, spaces)
    ]
    grp = groups.reshape(1, TERMS)
    payload, normal, dmat = fit(own, sum(others[1:], others[0]), grp)
    row = lax.broadcasted_iota(jnp.int32, payload.shape, 0)
    params = lax.axis_size("param")
    pieces = [payload]
    for k in range(1, shares):
        pieces.append(lax.ppermute(payload, "term", [((i + k) % shares, i) for i in range(shares)]))
    total = sum(pieces[1:], pieces[0])
    largest = functools.reduce(jnp.maximum, pieces)
    payload = jnp.where(row == 31, largest, total)
    pieces = [payload]
    for k in range(1, params):
        pieces.append(lax.ppermute(payload, "param", [((i + k) % params, i) for i in range(params)]))
    return end(grp, normal, dmat, pieces)


def solution(mesh):
    return jax.shard_map(
        body,
        mesh=mesh,
        in_specs=(P("param", None, None, "space", None), P("term", None), P(), P(), P(), P()),
        out_specs=(P(("param", "term"), None, None), P(("param", "term"), None, None)),
        check_vma=False,
    )
```

```python
import functools

import jax
import jax.numpy as jnp
from jax import lax
from jax.experimental import pallas as pl
from jax.experimental.pallas import tpu as pltpu
from jax.sharding import PartitionSpec as P

NX = 128
NY = 128
NT = 8
POWERS = 7
TERMS = 168
TESTS = 1024
KX = 16
KY = 16
KT = 4
RX = 16
RT = 4
GROUPS = 24
ROWS = 3 * KY
LANES = 4 * KT * KX
HALF = GROUPS // 2 + 1
WIDTH = 384
VMEM_LIMIT = 40 * 2**20

f32, bf16 = jnp.float32, jnp.bfloat16
NT_DIMS = ((1,), (1,))
NN_DIMS = ((1,), (0,))


def split(x):
    high = x.astype(bf16)
    return high, (x - high.astype(f32)).astype(bf16)


def dot(a, b, dims):
    return lax.dot_general(a, b, (dims, ((), ())), preferred_element_type=f32)


def dot3(a, b, dims):
    ah, al = split(a)
    bh, bl = split(b)
    return dot(ah, bh, dims) + (dot(ah, bl, dims) + dot(al, bh, dims))


def space_rows(offset):
    scaled = offset.astype(f32) * (1.0 / RX)
    base = 1.0 - scaled * scaled
    inside = jnp.abs(scaled) < 1.0
    cube = base * base * base
    value = jnp.where(inside, cube * base, 0.0)
    first = jnp.where(inside, 8.0 * scaled * cube * (1.0 / RX), 0.0)
    second = jnp.where(
        inside, -8.0 * (cube - 6.0 * scaled * scaled * base * base) * (1.0 / (RX * RX)), 0.0
    )
    return value, first, second


def integrals_kernel(
    rows, centers_x, centers_y, centers_t, fields, out,
    cx, cy, ct, pair, power_u, powers_v, y_split, tx_split, high, low, sem,
):
    cells = NT * rows
    first_row = lax.axis_index("space") * rows
    copy = pltpu.make_async_copy(fields.at[lax.axis_index("term")], pair, sem.at[0])
    small = [
        pltpu.make_async_copy(source, target, sem.at[1 + i])
        for i, (source, target) in enumerate(((centers_x, cx), (centers_y, cy), (centers_t, ct)))
    ]
    for one in small:
        one.start()
    copy.start()
    for one in small:
        one.wait()
    row = lax.broadcasted_iota(jnp.int32, (KY, NY), 0)
    lane = lax.broadcasted_iota(jnp.int32, (KY, NY), 1)
    center = jnp.zeros((KY, NY), jnp.int32)
    for k in range(KY):
        center = jnp.where(row == k, cy[k], center)
    offset = ((lane - center + NY // 2) & (NY - 1)) - NY // 2
    for i, part in enumerate(split(jnp.concatenate(space_rows(offset), axis=0))):
        y_split[pl.ds(i * ROWS, ROWS), :] = jnp.concatenate([part, part], axis=1)
    lane = lax.broadcasted_iota(jnp.int32, (1, LANES), 1)
    slot, kt, kx = lane >> 6, (lane >> 4) & 3, lane & 15
    center_x = jnp.zeros((1, LANES), jnp.int32)
    center_t = jnp.zeros((1, LANES), jnp.int32)
    for k in range(KX):
        center_x = jnp.where(kx == k, cx[k], center_x)
    for k in range(KT):
        center_t = jnp.where(kt == k, ct[k], center_t)
    row = lax.broadcasted_iota(jnp.int32, (rows, LANES), 0) + first_row
    offset = ((row - center_x + NX // 2) & (NX - 1)) - NX // 2
    value, first, second = space_rows(offset)
    x_table = jnp.where(slot == 1, first, jnp.where(slot == 2, second, value))
    for t in range(NT):
        scaled = (t - center_t).astype(f32) * (1.0 / RT)
        base = 1.0 - scaled * scaled
        weight = jnp.where(slot == 3, 4.0 * scaled * base * (1.0 / RT), base * base)
        weight = jnp.where(jnp.abs(scaled) < 1.0, weight, 0.0)
        for i, part in enumerate(split(x_table * weight)):
            tx_split[i, pl.ds(t * rows, rows), :] = part
    copy.wait()
    power_u[...] = jnp.ones((cells, NY), f32)
    v = pair[1].reshape(cells, NY)
    power = v
    powers_v[0] = v
    for b in range(1, POWERS - 1):
        power = power * v
        powers_v[b] = power
    tile = 256

    def one_power(a, _):
        for b in range(POWERS):
            for h in range(cells // tile):
                part = pl.ds(h * tile, tile)
                monomial = power_u[part, :]
                if b:
                    monomial = monomial * powers_v[b - 1, part, :]
                both = jnp.concatenate(split(monomial), axis=1)
                across = dot(y_split[...], both, NT_DIMS)
                across_high, across_low = split(across[:ROWS] + across[ROWS:])
                high[pl.ds(b * ROWS, ROWS), part] = across_high
                low[pl.ds(b * ROWS, ROWS), part] = across_low
        result = (
            dot(high[...], tx_split[0], NN_DIMS)
            + dot(low[...], tx_split[0], NN_DIMS)
            + dot(high[...], tx_split[1], NN_DIMS)
        )
        span = POWERS * ROWS
        place = pl.ds(pl.multiple_of(a * span, 8), span)
        out[0, place, :] = result[:, :128]
        out[1, place, :] = result[:, 128:]
        power_u[...] = power_u[...] * pair[0].reshape(cells, NY)
        return 0

    lax.fori_loop(0, POWERS, one_power, 0)


def integrals(cx, cy, ct, fields):
    rows = fields.shape[3]
    cells = NT * rows
    operands = [pltpu.with_memory_space_constraint(x, pltpu.HBM) for x in (cx, cy, ct, fields)]
    return pl.pallas_call(
        functools.partial(integrals_kernel, rows),
        out_shape=jax.ShapeDtypeStruct((2, POWERS * POWERS * ROWS, 128), f32),
        in_specs=[pl.BlockSpec(memory_space=pltpu.HBM)] * 4,
        out_specs=pl.BlockSpec(memory_space=pltpu.VMEM),
        scratch_shapes=[
            pltpu.SMEM((KX,), jnp.int32),
            pltpu.SMEM((KY,), jnp.int32),
            pltpu.SMEM((KT,), jnp.int32),
            pltpu.VMEM((2, NT, rows, NY), f32),
            pltpu.VMEM((cells, NY), f32),
            pltpu.VMEM((POWERS - 1, cells, NY), f32),
            pltpu.VMEM((2 * ROWS, 2 * NY), bf16),
            pltpu.VMEM((2, cells, LANES), bf16),
            pltpu.VMEM((POWERS * ROWS, cells), bf16),
            pltpu.VMEM((POWERS * ROWS, cells), bf16),
            pltpu.SemaphoreType.DMA((4,)),
        ],
        compiler_params=pltpu.CompilerParams(vmem_limit_bytes=VMEM_LIMIT),
        cost_estimate=pl.CostEstimate(flops=10**10, bytes_accessed=3 * 10**6, transcendentals=0),
        name="integrals",
    )(*operands)


def pick_kernel(local, shares, *refs):
    libs = refs[:shares]
    flat, out = refs[shares:]
    left = lax.broadcasted_iota(jnp.int32, (8, 128), 1) < 64
    me = lax.axis_index("term")

    def load(a, b, dx, dy):
        row = pl.multiple_of((a * POWERS + b) * ROWS + dy * KY, 8)
        chunk = dx >> 1
        return (dx & 1) == 1, flat[chunk, pl.ds(row, 8), :], flat[chunk, pl.ds(row + 8, 8), :]

    def store(j, odd, top, low):
        even_value = jnp.where(left, top, pltpu.roll(low, 64, 1))
        odd_value = jnp.where(left, pltpu.roll(top, 64, 1), low)
        out[pl.ds(pl.multiple_of(j * 8, 8), 8), :] = jnp.where(odd, odd_value, even_value)

    batch = max(n for n in range(1, 22) if local % n == 0)
    for k in range(shares):
        first = lax.rem(me + k, shares) * local
        lib = libs[k]

        def some(i, _):
            loaded = [
                load(*(lib[part, i * batch + n] for part in range(4))) for n in range(batch)
            ]
            for n in range(batch):
                store(first + i * batch + n, *loaded[n])
            return 0

        lax.fori_loop(0, local // batch, some, 0)
    store(TERMS, *load(1, 0, 3, 0))
    store(TERMS + 1, *load(0, 1, 3, 0))
    out[pl.ds((TERMS + 2) * 8, 48), :] = jnp.zeros((48, 128), f32)


def pick(libs, flat):
    shares = len(libs)
    smem = pl.BlockSpec(memory_space=pltpu.SMEM)
    vmem = pl.BlockSpec(memory_space=pltpu.VMEM)
    return pl.pallas_call(
        functools.partial(pick_kernel, libs[0].shape[1], shares),
        out_shape=jax.ShapeDtypeStruct(((TERMS + 8) * 8, 128), f32),
        in_specs=[smem] * shares + [vmem],
        out_specs=vmem,
        compiler_params=pltpu.CompilerParams(vmem_limit_bytes=VMEM_LIMIT),
        name="pick",
    )(*libs, flat)


def fit_kernel(own, other, grp, payload, normal, dmat):
    pad = TERMS + 8
    gram = jnp.zeros((pad, pad), f32)
    for q in range(4):
        parts = []
        for s in (2 * q, 2 * q + 1):
            rows = pl.ds(s, pad, stride=8)
            parts.append(own[rows, :] + other[rows, :])
        x = jnp.concatenate(parts, axis=1)
        gram = gram + dot3(x, x, NT_DIMS)
    ri = lax.broadcasted_iota(jnp.int32, (pad, pad), 0)
    ci = lax.broadcasted_iota(jnp.int32, (pad, pad), 1)
    diagonal = jnp.where(ri == ci, gram, 0.0)
    dcol = jnp.sum(diagonal, axis=1, keepdims=True)
    drow = jnp.sum(diagonal, axis=0, keepdims=True)
    icol = 1.0 / jnp.sqrt(dcol * (1.0 / TESTS) + 1e-06)
    irow = 1.0 / jnp.sqrt(drow * (1.0 / TESTS) + 1e-06)
    norm = (gram * (icol * (1.0 / TESTS))) * irow
    norm = jnp.where(ci < TERMS, norm, 0.0)
    corr = norm[:TERMS, :TERMS]
    squares = jnp.sum(jnp.sum(corr * corr, axis=0, keepdims=True), axis=1, keepdims=True)
    normal[...] = norm[:, :TERMS]
    gi = lax.broadcasted_iota(jnp.int32, (GROUPS, TERMS), 0)
    onehot = gi == grp[...]
    products = [0.0] * (HALF + 2)
    for s in range(2):
        right = norm[TERMS + s : TERMS + s + 1, :TERMS]
        d = dot3(jnp.where(onehot, right, 0.0), corr, NN_DIMS)
        dmat[pl.ds(s * GROUPS, GROUPS), :] = d
        products[0] = products[0] + d * d
        for shift in range(1, HALF):
            products[shift] = products[shift] + d * jnp.concatenate([d[shift:], d[:shift]], axis=0)
        products[HALF] = products[HALF] + d * right
        products[HALF + 1] = products[HALF + 1] + right * right
    used = HALF * GROUPS + GROUPS + 1
    products[HALF + 1] = jnp.concatenate(
        [products[HALF + 1], jnp.zeros((WIDTH - used, TERMS), f32)], axis=0
    )
    high, low = split(jnp.concatenate(products, axis=0))
    members = onehot.astype(f32).astype(bf16)
    sums = dot(members, high, NT_DIMS) + dot(members, low, NT_DIMS)
    col = lax.broadcasted_iota(jnp.int32, (GROUPS, WIDTH), 1)
    payload[...] = jnp.where(col == WIDTH - 1, squares, sums)


def fit(own, other, grp):
    vmem = pl.BlockSpec(memory_space=pltpu.VMEM)
    return pl.pallas_call(
        fit_kernel,
        out_shape=(
            jax.ShapeDtypeStruct((GROUPS, WIDTH), f32),
            jax.ShapeDtypeStruct((TERMS + 8, TERMS), f32),
            jax.ShapeDtypeStruct((2 * GROUPS, TERMS), f32),
        ),
        in_specs=[vmem] * 3,
        out_specs=(vmem,) * 3,
        compiler_params=pltpu.CompilerParams(vmem_limit_bytes=VMEM_LIMIT),
        name="fit",
    )(own, other, grp)


def end_kernel(shares, grp, normal, dmat, *refs):
    pieces = refs[:shares]
    coef, misfit = refs[shares:]
    total = pieces[0][...]
    largest = total[:1, WIDTH - 1 :]
    for piece in pieces[1:]:
        value = piece[...]
        total = total + value
        largest = jnp.maximum(largest, value[:1, WIDTH - 1 :])
    step = 1.0 / jnp.sqrt(largest)
    first = HALF * GROUPS

    def factor(totals):
        threshold = 0.7 * jnp.sqrt(jnp.sum(totals, axis=0, keepdims=True) * (1.0 / GROUPS))
        return jnp.maximum(0.0, 1.0 - threshold / jnp.sqrt(totals + 1e-12))

    squares = total[:, first + GROUPS : first + GROUPS + 1]
    f_col = factor(step * step * squares)
    col = lax.broadcasted_iota(jnp.int32, (GROUPS, WIDTH), 1)
    group = lax.broadcasted_iota(jnp.int32, (GROUPS, WIDTH), 0)
    shift = jnp.zeros((GROUPS, WIDTH), jnp.int32)
    for k in range(1, HALF + 1):
        shift = jnp.where(col >= k * GROUPS, k, shift)
    one = col - shift * GROUPS
    two = one + shift
    two = jnp.where(two >= GROUPS, two - GROUPS, two)
    f_one = jnp.sum(jnp.where(group == one, f_col, 0.0), axis=0, keepdims=True)
    f_two = jnp.sum(jnp.where(group == two, f_col, 0.0), axis=0, keepdims=True)
    col, shift = col[:1], shift[:1]
    twice = jnp.where((shift == 0) | (shift == HALF - 1), 1.0, 2.0)
    pairs = jnp.where(col < first, twice * f_one * f_two, 0.0)
    singles = jnp.where((col >= first) & (col < first + GROUPS), f_one, 0.0)
    quad = jnp.sum(total * pairs, axis=1, keepdims=True)
    cross = jnp.sum(total * singles, axis=1, keepdims=True)
    grow = 1.0 + f_col
    totals = grow * grow * squares - 2.0 * step * grow * cross + step * step * quad
    f2_col = factor(jnp.maximum(step * step * totals, 0.0))
    term_group = lax.broadcasted_iota(jnp.int32, (GROUPS, TERMS), 0)
    onehot = term_group == grp[...]
    f_term = jnp.sum(jnp.where(onehot, f_col, 0.0), axis=0, keepdims=True)
    f2_term = jnp.sum(jnp.where(onehot, f2_col, 0.0), axis=0, keepdims=True)
    seconds = []
    for s in range(2):
        right = normal[pl.ds(TERMS + s, 1), :]
        pulled = jnp.sum(dmat[pl.ds(s * GROUPS, GROUPS), :] * f_col, axis=0, keepdims=True)
        seconds.append(step * ((1.0 + f_term) * right - step * pulled) * f2_term)
    second = jnp.concatenate(seconds + [jnp.zeros((6, TERMS), f32)], axis=0)
    coef[0] = (second / step)[:2]
    moved = dot3(second, normal[pl.ds(0, TERMS), :], NN_DIMS)
    misfit[0] = normal[pl.ds(TERMS, 2), :] - moved[:2]


def end(grp, normal, dmat, pieces):
    vmem = pl.BlockSpec(memory_space=pltpu.VMEM)
    shape = jax.ShapeDtypeStruct((1, 2, TERMS), f32)
    return pl.pallas_call(
        functools.partial(end_kernel, len(pieces)),
        out_shape=(shape, shape),
        in_specs=[vmem] * (3 + len(pieces)),
        out_specs=(vmem, vmem),
        compiler_params=pltpu.CompilerParams(vmem_limit_bytes=VMEM_LIMIT),
        name="finish",
    )(grp, normal, dmat, *pieces)


def body(fields, library, centers_x, centers_y, centers_t, groups):
    pgroup = fields.shape[0]
    shares = lax.axis_size("term")
    local = library.shape[0]
    library = library.T
    if pgroup != shares or local * shares != TERMS:
        raise ValueError("unexpected split")
    libs = [library]
    for k in range(1, shares):
        libs.append(lax.ppermute(library, "term", [((i + k) % shares, i) for i in range(shares)]))
    flat = integrals(centers_x, centers_y, centers_t, fields)
    own = pick(libs, flat)
    spaces = lax.axis_size("space")
    others = [
        lax.ppermute(own, "space", [((i + k) % spaces, i) for i in range(spaces)])
        for k in range(1, spaces)
    ]
    grp = groups.reshape(1, TERMS)
    payload, normal, dmat = fit(own, sum(others[1:], others[0]), grp)
    col = lax.broadcasted_iota(jnp.int32, payload.shape, 1)
    params = lax.axis_size("param")
    pieces = [payload]
    for k in range(1, shares):
        pieces.append(lax.ppermute(payload, "term", [((i + k) % shares, i) for i in range(shares)]))
    total = sum(pieces[1:], pieces[0])
    largest = functools.reduce(jnp.maximum, pieces)
    payload = jnp.where(col == WIDTH - 1, largest, total)
    pieces = [payload]
    for k in range(1, params):
        pieces.append(lax.ppermute(payload, "param", [((i + k) % params, i) for i in range(params)]))
    return end(grp, normal, dmat, pieces)


def solution(mesh):
    return jax.shard_map(
        body,
        mesh=mesh,
        in_specs=(P("param", None, None, "space", None), P("term", None), P(), P(), P(), P()),
        out_specs=(P(("param", "term"), None, None), P(("param", "term"), None, None)),
        check_vma=False,
    )
```

```python
import functools

import jax
import jax.numpy as jnp
from jax import lax
from jax.experimental import pallas as pl
from jax.experimental.pallas import tpu as pltpu
from jax.sharding import PartitionSpec as P

NX = 128
NY = 128
NT = 8
POWERS = 7
TERMS = 168
TESTS = 1024
KX = 16
KY = 16
KT = 4
RX = 16
RT = 4
GROUPS = 24
ROWS = 3 * KY
LANES = 4 * KT * KX
HALF = GROUPS // 2 + 1
WIDTH = 384
VMEM_LIMIT = 40 * 2**20

f32, bf16 = jnp.float32, jnp.bfloat16
NT_DIMS = ((1,), (1,))
NN_DIMS = ((1,), (0,))


def split(x):
    high = x.astype(bf16)
    return high, (x - high.astype(f32)).astype(bf16)


def dot(a, b, dims):
    return lax.dot_general(a, b, (dims, ((), ())), preferred_element_type=f32)


def dot3(a, b, dims):
    ah, al = split(a)
    bh, bl = split(b)
    return dot(ah, bh, dims) + (dot(ah, bl, dims) + dot(al, bh, dims))


def space_rows(offset):
    scaled = offset.astype(f32) * (1.0 / RX)
    base = 1.0 - scaled * scaled
    inside = jnp.abs(scaled) < 1.0
    cube = base * base * base
    value = jnp.where(inside, cube * base, 0.0)
    first = jnp.where(inside, 8.0 * scaled * cube * (1.0 / RX), 0.0)
    second = jnp.where(
        inside, -8.0 * (cube - 6.0 * scaled * scaled * base * base) * (1.0 / (RX * RX)), 0.0
    )
    return value, first, second


def integrals_kernel(
    rows, centers_x, centers_y, centers_t, fields, out,
    cx, cy, ct, pair, u_cells, power_u, powers_v, y_split, tx_split, high, low, sem,
):
    cells = NT * rows
    first_row = lax.axis_index("space") * rows
    copy = pltpu.make_async_copy(fields.at[lax.axis_index("term")], pair, sem.at[0])
    small = [
        pltpu.make_async_copy(source, target, sem.at[1 + i])
        for i, (source, target) in enumerate(((centers_x, cx), (centers_y, cy), (centers_t, ct)))
    ]
    for one in small:
        one.start()
    copy.start()
    for one in small:
        one.wait()
    row = lax.broadcasted_iota(jnp.int32, (KY, NY), 0)
    lane = lax.broadcasted_iota(jnp.int32, (KY, NY), 1)
    center = jnp.zeros((KY, NY), jnp.int32)
    for k in range(KY):
        center = jnp.where(row == k, cy[k], center)
    offset = ((lane - center + NY // 2) & (NY - 1)) - NY // 2
    for i, part in enumerate(split(jnp.concatenate(space_rows(offset), axis=0))):
        y_split[pl.ds(i * ROWS, ROWS), :] = jnp.concatenate([part, part], axis=1)
    lane = lax.broadcasted_iota(jnp.int32, (1, LANES), 1)
    slot, kt, kx = lane >> 6, (lane >> 4) & 3, lane & 15
    center_x = jnp.zeros((1, LANES), jnp.int32)
    center_t = jnp.zeros((1, LANES), jnp.int32)
    for k in range(KX):
        center_x = jnp.where(kx == k, cx[k], center_x)
    for k in range(KT):
        center_t = jnp.where(kt == k, ct[k], center_t)
    row = lax.broadcasted_iota(jnp.int32, (rows, LANES), 0) + first_row
    offset = ((row - center_x + NX // 2) & (NX - 1)) - NX // 2
    value, first, second = space_rows(offset)
    x_table = jnp.where(slot == 1, first, jnp.where(slot == 2, second, value))
    for t in range(NT):
        scaled = (t - center_t).astype(f32) * (1.0 / RT)
        base = 1.0 - scaled * scaled
        weight = jnp.where(slot == 3, 4.0 * scaled * base * (1.0 / RT), base * base)
        weight = jnp.where(jnp.abs(scaled) < 1.0, weight, 0.0)
        for i, part in enumerate(split(x_table * weight)):
            tx_split[i, pl.ds(t * rows, rows), :] = part
    copy.wait()
    power_u[...] = jnp.ones((NY, cells), f32)
    u_cells[...] = pair[0].reshape(cells, NY).T
    v = pair[1].reshape(cells, NY).T
    power = v
    powers_v[0] = v
    for b in range(1, POWERS - 1):
        power = power * v
        powers_v[b] = power
    tile = 256

    def one_power(a, _):
        for b in range(POWERS):
            for h in range(cells // tile):
                part = pl.ds(h * tile, tile)
                monomial = power_u[:, part]
                if b:
                    monomial = monomial * powers_v[b - 1, :, part]
                both = jnp.concatenate(split(monomial), axis=0)
                across = dot(y_split[...], both, NN_DIMS)
                across_high, across_low = split(across[:ROWS] + across[ROWS:])
                high[pl.ds(b * ROWS, ROWS), part] = across_high
                low[pl.ds(b * ROWS, ROWS), part] = across_low
        result = (
            dot(high[...], tx_split[0], NN_DIMS)
            + dot(low[...], tx_split[0], NN_DIMS)
            + dot(high[...], tx_split[1], NN_DIMS)
        )
        span = POWERS * ROWS
        place = pl.ds(pl.multiple_of(a * span, 8), span)
        out[0, place, :] = result[:, :128]
        out[1, place, :] = result[:, 128:]
        power_u[...] = power_u[...] * u_cells[...]
        return 0

    lax.fori_loop(0, POWERS, one_power, 0)


def integrals(cx, cy, ct, fields):
    rows = fields.shape[3]
    cells = NT * rows
    operands = [pltpu.with_memory_space_constraint(x, pltpu.HBM) for x in (cx, cy, ct, fields)]
    return pl.pallas_call(
        functools.partial(integrals_kernel, rows),
        out_shape=jax.ShapeDtypeStruct((2, POWERS * POWERS * ROWS, 128), f32),
        in_specs=[pl.BlockSpec(memory_space=pltpu.HBM)] * 4,
        out_specs=pl.BlockSpec(memory_space=pltpu.VMEM),
        scratch_shapes=[
            pltpu.SMEM((KX,), jnp.int32),
            pltpu.SMEM((KY,), jnp.int32),
            pltpu.SMEM((KT,), jnp.int32),
            pltpu.VMEM((2, NT, rows, NY), f32),
            pltpu.VMEM((NY, cells), f32),
            pltpu.VMEM((NY, cells), f32),
            pltpu.VMEM((POWERS - 1, NY, cells), f32),
            pltpu.VMEM((2 * ROWS, 2 * NY), bf16),
            pltpu.VMEM((2, cells, LANES), bf16),
            pltpu.VMEM((POWERS * ROWS, cells), bf16),
            pltpu.VMEM((POWERS * ROWS, cells), bf16),
            pltpu.SemaphoreType.DMA((4,)),
        ],
        compiler_params=pltpu.CompilerParams(vmem_limit_bytes=VMEM_LIMIT),
        cost_estimate=pl.CostEstimate(flops=10**10, bytes_accessed=3 * 10**6, transcendentals=0),
        name="integrals",
    )(*operands)


def pick_kernel(local, *refs):
    *libs, flat, out = refs
    left = lax.broadcasted_iota(jnp.int32, (8, 128), 1) < 64
    me = lax.axis_index("term")

    def load(a, b, dx, dy):
        row = pl.multiple_of((a * POWERS + b) * ROWS + dy * KY, 8)
        chunk = dx >> 1
        return (dx & 1) == 1, flat[chunk, pl.ds(row, 8), :], flat[chunk, pl.ds(row + 8, 8), :]

    def store(j, odd, top, low):
        even_value = jnp.where(left, top, pltpu.roll(low, 64, 1))
        odd_value = jnp.where(left, pltpu.roll(top, 64, 1), low)
        out[pl.ds(pl.multiple_of(j * 8, 8), 8), :] = jnp.where(odd, odd_value, even_value)

    done = 0
    for lib in libs:
        for k in range(lib.shape[0] // 4):
            first = (me ^ done) * local
            loaded = [load(*(lib[4 * k + part, n] for part in range(4))) for n in range(local)]
            for n in range(local):
                store(first + n, *loaded[n])
            done += 1
    store(TERMS, *load(1, 0, 3, 0))
    store(TERMS + 1, *load(0, 1, 3, 0))
    out[pl.ds((TERMS + 2) * 8, 48), :] = jnp.zeros((48, 128), f32)


def pick(libs, flat):
    smem = pl.BlockSpec(memory_space=pltpu.SMEM)
    vmem = pl.BlockSpec(memory_space=pltpu.VMEM)
    return pl.pallas_call(
        functools.partial(pick_kernel, libs[0].shape[1]),
        out_shape=jax.ShapeDtypeStruct(((TERMS + 8) * 8, 128), f32),
        in_specs=[smem] * len(libs) + [vmem],
        out_specs=vmem,
        compiler_params=pltpu.CompilerParams(vmem_limit_bytes=VMEM_LIMIT),
        name="pick",
    )(*libs, flat)


def fit_kernel(own, other, grp, payload, normal, dmat):
    pad = TERMS + 8
    gram = jnp.zeros((pad, pad), f32)
    for q in range(4):
        parts = []
        for s in (2 * q, 2 * q + 1):
            rows = pl.ds(s, pad, stride=8)
            parts.append(own[rows, :] + other[rows, :])
        x = jnp.concatenate(parts, axis=1)
        gram = gram + dot3(x, x, NT_DIMS)
    ri = lax.broadcasted_iota(jnp.int32, (pad, pad), 0)
    ci = lax.broadcasted_iota(jnp.int32, (pad, pad), 1)
    diagonal = jnp.where(ri == ci, gram, 0.0)
    dcol = jnp.sum(diagonal, axis=1, keepdims=True)
    drow = jnp.sum(diagonal, axis=0, keepdims=True)
    icol = 1.0 / jnp.sqrt(dcol * (1.0 / TESTS) + 1e-06)
    irow = 1.0 / jnp.sqrt(drow * (1.0 / TESTS) + 1e-06)
    norm = (gram * (icol * (1.0 / TESTS))) * irow
    norm = jnp.where(ci < TERMS, norm, 0.0)
    corr = norm[:TERMS, :TERMS]
    squares = jnp.sum(jnp.sum(corr * corr, axis=0, keepdims=True), axis=1, keepdims=True)
    normal[...] = norm[:, :TERMS]
    gi = lax.broadcasted_iota(jnp.int32, (GROUPS, TERMS), 0)
    onehot = gi == grp[...]
    products = [0.0] * (HALF + 2)
    for s in range(2):
        right = norm[TERMS + s : TERMS + s + 1, :TERMS]
        d = dot3(jnp.where(onehot, right, 0.0), corr, NN_DIMS)
        dmat[pl.ds(s * GROUPS, GROUPS), :] = d
        products[0] = products[0] + d * d
        for shift in range(1, HALF):
            products[shift] = products[shift] + d * jnp.concatenate([d[shift:], d[:shift]], axis=0)
        products[HALF] = products[HALF] + d * right
        products[HALF + 1] = products[HALF + 1] + right * right
    used = HALF * GROUPS + GROUPS + 1
    products[HALF + 1] = jnp.concatenate(
        [products[HALF + 1], jnp.zeros((WIDTH - used, TERMS), f32)], axis=0
    )
    high, low = split(jnp.concatenate(products, axis=0))
    members = onehot.astype(f32).astype(bf16)
    sums = dot(members, high, NT_DIMS) + dot(members, low, NT_DIMS)
    col = lax.broadcasted_iota(jnp.int32, (GROUPS, WIDTH), 1)
    payload[...] = jnp.where(col == WIDTH - 1, squares, sums)


def fit(own, other, grp):
    vmem = pl.BlockSpec(memory_space=pltpu.VMEM)
    return pl.pallas_call(
        fit_kernel,
        out_shape=(
            jax.ShapeDtypeStruct((GROUPS, WIDTH), f32),
            jax.ShapeDtypeStruct((TERMS + 8, TERMS), f32),
            jax.ShapeDtypeStruct((2 * GROUPS, TERMS), f32),
        ),
        in_specs=[vmem] * 3,
        out_specs=(vmem,) * 3,
        compiler_params=pltpu.CompilerParams(vmem_limit_bytes=VMEM_LIMIT),
        name="fit",
    )(own, other, grp)


def end_kernel(shares, grp, normal, dmat, *refs):
    pieces = refs[:shares]
    coef, misfit = refs[shares:]
    total = pieces[0][...]
    largest = total[:1, WIDTH - 1 :]
    for piece in pieces[1:]:
        value = piece[...]
        total = total + value
        largest = jnp.maximum(largest, value[:1, WIDTH - 1 :])
    step = 1.0 / jnp.sqrt(largest)
    first = HALF * GROUPS

    def factor(totals):
        threshold = 0.7 * jnp.sqrt(jnp.sum(totals, axis=0, keepdims=True) * (1.0 / GROUPS))
        return jnp.maximum(0.0, 1.0 - threshold / jnp.sqrt(totals + 1e-12))

    squares = total[:, first + GROUPS : first + GROUPS + 1]
    f_col = factor(step * step * squares)
    col = lax.broadcasted_iota(jnp.int32, (GROUPS, WIDTH), 1)
    group = lax.broadcasted_iota(jnp.int32, (GROUPS, WIDTH), 0)
    shift = jnp.zeros((GROUPS, WIDTH), jnp.int32)
    for k in range(1, HALF + 1):
        shift = jnp.where(col >= k * GROUPS, k, shift)
    one = col - shift * GROUPS
    two = one + shift
    two = jnp.where(two >= GROUPS, two - GROUPS, two)
    f_one = jnp.sum(jnp.where(group == one, f_col, 0.0), axis=0, keepdims=True)
    f_two = jnp.sum(jnp.where(group == two, f_col, 0.0), axis=0, keepdims=True)
    col, shift = col[:1], shift[:1]
    twice = jnp.where((shift == 0) | (shift == HALF - 1), 1.0, 2.0)
    pairs = jnp.where(col < first, twice * f_one * f_two, 0.0)
    singles = jnp.where((col >= first) & (col < first + GROUPS), f_one, 0.0)
    quad = jnp.sum(total * pairs, axis=1, keepdims=True)
    cross = jnp.sum(total * singles, axis=1, keepdims=True)
    grow = 1.0 + f_col
    totals = grow * grow * squares - 2.0 * step * grow * cross + step * step * quad
    f2_col = factor(jnp.maximum(step * step * totals, 0.0))
    term_group = lax.broadcasted_iota(jnp.int32, (GROUPS, TERMS), 0)
    onehot = term_group == grp[...]
    f_term = jnp.sum(jnp.where(onehot, f_col, 0.0), axis=0, keepdims=True)
    f2_term = jnp.sum(jnp.where(onehot, f2_col, 0.0), axis=0, keepdims=True)
    seconds = []
    for s in range(2):
        right = normal[pl.ds(TERMS + s, 1), :]
        pulled = jnp.sum(dmat[pl.ds(s * GROUPS, GROUPS), :] * f_col, axis=0, keepdims=True)
        seconds.append(step * ((1.0 + f_term) * right - step * pulled) * f2_term)
    second = jnp.concatenate(seconds + [jnp.zeros((6, TERMS), f32)], axis=0)
    coef[0] = (second / step)[:2]
    moved = dot3(second, normal[pl.ds(0, TERMS), :], NN_DIMS)
    misfit[0] = normal[pl.ds(TERMS, 2), :] - moved[:2]


def end(grp, normal, dmat, pieces):
    vmem = pl.BlockSpec(memory_space=pltpu.VMEM)
    shape = jax.ShapeDtypeStruct((1, 2, TERMS), f32)
    return pl.pallas_call(
        functools.partial(end_kernel, len(pieces)),
        out_shape=(shape, shape),
        in_specs=[vmem] * (3 + len(pieces)),
        out_specs=(vmem, vmem),
        compiler_params=pltpu.CompilerParams(vmem_limit_bytes=VMEM_LIMIT),
        name="finish",
    )(grp, normal, dmat, *pieces)


def partner(index, k, size):
    return index ^ k if size & (size - 1) == 0 else (index + k) % size


def neighbour_last(size):
    return (*range(2, size), 1) if size > 1 else ()


def exchange(value, axis, k):
    size = lax.axis_size(axis)
    return lax.ppermute(value, axis, [(partner(i, k, size), i) for i in range(size)])


def body(fields, library, centers_x, centers_y, centers_t, groups):
    pgroup = fields.shape[0]
    shares = lax.axis_size("term")
    local = library.shape[0]
    library = library.T
    if pgroup != shares or local * shares != TERMS or shares & (shares - 1):
        raise ValueError("unexpected split")
    libs = [library] + [exchange(library, "term", k) for k in range(1, shares)]
    flat = integrals(centers_x, centers_y, centers_t, fields)
    own = pick(libs, flat)
    spaces = lax.axis_size("space")
    others = [exchange(own, "space", k) for k in range(1, spaces)]
    grp = groups.reshape(1, TERMS)
    payload, normal, dmat = fit(own, sum(others[1:], others[0]), grp)
    col = lax.broadcasted_iota(jnp.int32, payload.shape, 1)
    params = lax.axis_size("param")
    pieces = [payload]
    for k in neighbour_last(shares):
        pieces.append(exchange(payload, "term", k))
    total = sum(pieces[1:], pieces[0])
    largest = functools.reduce(jnp.maximum, pieces)
    payload = jnp.where(col == WIDTH - 1, largest, total)
    pieces = [payload]
    for k in neighbour_last(params):
        pieces.append(exchange(payload, "param", k))
    return end(grp, normal, dmat, pieces)


def solution(mesh):
    return jax.shard_map(
        body,
        mesh=mesh,
        in_specs=(P("param", None, None, "space", None), P("term", None), P(), P(), P(), P()),
        out_specs=(P(("param", "term"), None, None), P(("param", "term"), None, None)),
        check_vma=False,
    )
```

```python
import functools

import jax
import jax.numpy as jnp
from jax import lax
from jax.experimental import pallas as pl
from jax.experimental.pallas import tpu as pltpu
from jax.sharding import PartitionSpec as P

NX = 128
NY = 128
NT = 8
POWERS = 7
TERMS = 168
TESTS = 1024
KX = 16
KY = 16
KT = 4
RX = 16
RT = 4
GROUPS = 24
ROWS = 3 * KY
LANES = 4 * KT * KX
HALF = GROUPS // 2 + 1
WIDTH = 384
VMEM_LIMIT = 40 * 2**20

f32, bf16 = jnp.float32, jnp.bfloat16
NT_DIMS = ((1,), (1,))
NN_DIMS = ((1,), (0,))


def split(x):
    high = x.astype(bf16)
    return high, (x - high.astype(f32)).astype(bf16)


def dot(a, b, dims):
    return lax.dot_general(a, b, (dims, ((), ())), preferred_element_type=f32)


def dot3(a, b, dims):
    ah, al = split(a)
    bh, bl = split(b)
    return dot(ah, bh, dims) + (dot(ah, bl, dims) + dot(al, bh, dims))


def space_rows(offset):
    scaled = offset.astype(f32) * (1.0 / RX)
    base = 1.0 - scaled * scaled
    inside = jnp.abs(scaled) < 1.0
    cube = base * base * base
    value = jnp.where(inside, cube * base, 0.0)
    first = jnp.where(inside, 8.0 * scaled * cube * (1.0 / RX), 0.0)
    second = jnp.where(
        inside, -8.0 * (cube - 6.0 * scaled * scaled * base * base) * (1.0 / (RX * RX)), 0.0
    )
    return value, first, second


def integrals_kernel(
    rows, centers_x, centers_y, centers_t, fields, out,
    cx, cy, ct, pair, u_cells, power_u, powers_v, y_split, tx_split, high, low, sem,
):
    cells = NT * rows
    first_row = lax.axis_index("space") * rows
    copy = pltpu.make_async_copy(fields.at[lax.axis_index("term")], pair, sem.at[0])
    small = [
        pltpu.make_async_copy(source, target, sem.at[1 + i])
        for i, (source, target) in enumerate(((centers_x, cx), (centers_y, cy), (centers_t, ct)))
    ]
    for one in small:
        one.start()
    copy.start()
    for one in small:
        one.wait()
    row = lax.broadcasted_iota(jnp.int32, (KY, NY), 0)
    lane = lax.broadcasted_iota(jnp.int32, (KY, NY), 1)
    center = jnp.zeros((KY, NY), jnp.int32)
    for k in range(KY):
        center = jnp.where(row == k, cy[k], center)
    offset = ((lane - center + NY // 2) & (NY - 1)) - NY // 2
    for i, part in enumerate(split(jnp.concatenate(space_rows(offset), axis=0))):
        y_split[pl.ds(i * ROWS, ROWS), :] = jnp.concatenate([part, part], axis=1)
    lane = lax.broadcasted_iota(jnp.int32, (1, LANES), 1)
    slot, kt, kx = lane >> 6, (lane >> 4) & 3, lane & 15
    center_x = jnp.zeros((1, LANES), jnp.int32)
    center_t = jnp.zeros((1, LANES), jnp.int32)
    for k in range(KX):
        center_x = jnp.where(kx == k, cx[k], center_x)
    for k in range(KT):
        center_t = jnp.where(kt == k, ct[k], center_t)
    row = lax.broadcasted_iota(jnp.int32, (rows, LANES), 0) + first_row
    offset = ((row - center_x + NX // 2) & (NX - 1)) - NX // 2
    value, first, second = space_rows(offset)
    x_table = jnp.where(slot == 1, first, jnp.where(slot == 2, second, value))
    for t in range(NT):
        scaled = (t - center_t).astype(f32) * (1.0 / RT)
        base = 1.0 - scaled * scaled
        weight = jnp.where(slot == 3, 4.0 * scaled * base * (1.0 / RT), base * base)
        weight = jnp.where(jnp.abs(scaled) < 1.0, weight, 0.0)
        for i, part in enumerate(split(x_table * weight)):
            tx_split[i, pl.ds(t * rows, rows), :] = part
    copy.wait()
    u = pair[0].reshape(cells, NY).T
    v = pair[1].reshape(cells, NY).T
    power_u[...] = u
    u_cells[...] = u
    power = v
    powers_v[0] = v
    for b in range(1, POWERS - 1):
        power = power * v
        powers_v[b] = power
    tile = 256
    span = POWERS * ROWS

    def contract(a):
        result = (
            dot(high[a & 1], tx_split[0], NN_DIMS)
            + dot(low[a & 1], tx_split[0], NN_DIMS)
            + dot(high[a & 1], tx_split[1], NN_DIMS)
        )
        out[0, pl.ds(a * span, span), :] = result[:, :128]
        out[1, pl.ds(a * span, span), :] = result[:, 128:]

    for a in range(POWERS):
        if a > 1:
            power_u[...] = power_u[...] * u_cells[...]
        for b in range(POWERS):
            for h in range(cells // tile):
                part = pl.ds(h * tile, tile)
                factors = ([power_u[:, part]] if a else []) + ([powers_v[b - 1, :, part]] if b else [])
                monomial = factors[0] if factors else jnp.ones((NY, tile), f32)
                if len(factors) > 1:
                    monomial = monomial * factors[1]
                both = jnp.concatenate(split(monomial), axis=0)
                across = dot(y_split[...], both, NN_DIMS)
                across_high, across_low = split(across[:ROWS] + across[ROWS:])
                high[a & 1, pl.ds( b * ROWS, ROWS), part] = across_high
                low[a & 1, pl.ds( b * ROWS, ROWS), part] = across_low
        if a: contract(a - 1)
    contract(POWERS - 1)


def integrals(cx, cy, ct, fields):
    rows = fields.shape[3]
    cells = NT * rows
    operands = [pltpu.with_memory_space_constraint(x, pltpu.HBM) for x in (cx, cy, ct, fields)]
    return pl.pallas_call(
        functools.partial(integrals_kernel, rows),
        out_shape=jax.ShapeDtypeStruct((2, POWERS * POWERS * ROWS, 128), f32),
        in_specs=[pl.BlockSpec(memory_space=pltpu.HBM)] * 4,
        out_specs=pl.BlockSpec(memory_space=pltpu.VMEM),
        scratch_shapes=[
            pltpu.SMEM((KX,), jnp.int32),
            pltpu.SMEM((KY,), jnp.int32),
            pltpu.SMEM((KT,), jnp.int32),
            pltpu.VMEM((2, NT, rows, NY), f32),
            pltpu.VMEM((NY, cells), f32),
            pltpu.VMEM((NY, cells), f32),
            pltpu.VMEM((POWERS - 1, NY, cells), f32),
            pltpu.VMEM((2 * ROWS, 2 * NY), bf16),
            pltpu.VMEM((2, cells, LANES), bf16),
            pltpu.VMEM((2, POWERS * ROWS, cells), bf16),
            pltpu.VMEM((2, POWERS * ROWS, cells), bf16),
            pltpu.SemaphoreType.DMA((4,)),
        ],
        compiler_params=pltpu.CompilerParams(vmem_limit_bytes=VMEM_LIMIT),
        cost_estimate=pl.CostEstimate(flops=10**10, bytes_accessed=3 * 10**6, transcendentals=0),
        name="integrals",
    )(*operands)


def pick_kernel(local, *refs):
    *libs, flat, out = refs
    left = lax.broadcasted_iota(jnp.int32, (8, 128), 1) < 64
    me = lax.axis_index("term")

    def load(a, b, dx, dy):
        row = pl.multiple_of((a * POWERS + b) * ROWS + dy * KY, 8)
        chunk = dx >> 1
        return (dx & 1) == 1, flat[chunk, pl.ds(row, 8), :], flat[chunk, pl.ds(row + 8, 8), :]

    def store(j, odd, top, low):
        even_value = jnp.where(left, top, pltpu.roll(low, 64, 1))
        odd_value = jnp.where(left, pltpu.roll(top, 64, 1), low)
        out[pl.ds(pl.multiple_of(j * 8, 8), 8), :] = jnp.where(odd, odd_value, even_value)

    done = 0
    for lib in libs:
        for k in range(lib.shape[0] // 4):
            first = (me ^ done) * local
            loaded = [load(*(lib[4 * k + part, n] for part in range(4))) for n in range(local)]
            for n in range(local):
                store(first + n, *loaded[n])
            done += 1
    store(TERMS, *load(1, 0, 3, 0))
    store(TERMS + 1, *load(0, 1, 3, 0))
    out[pl.ds((TERMS + 2) * 8, 48), :] = jnp.zeros((48, 128), f32)


def pick(libs, flat):
    smem = pl.BlockSpec(memory_space=pltpu.SMEM)
    vmem = pl.BlockSpec(memory_space=pltpu.VMEM)
    return pl.pallas_call(
        functools.partial(pick_kernel, libs[0].shape[1]),
        out_shape=jax.ShapeDtypeStruct(((TERMS + 8) * 8, 128), f32),
        in_specs=[smem] * len(libs) + [vmem],
        out_specs=vmem,
        compiler_params=pltpu.CompilerParams(vmem_limit_bytes=VMEM_LIMIT),
        name="pick",
    )(*libs, flat)


def fit_kernel(own, other, grp, payload, normal, dmat):
    pad = TERMS + 8
    gram = jnp.zeros((pad, pad), f32)
    for q in range(4):
        parts = []
        for s in (2 * q, 2 * q + 1):
            rows = pl.ds(s, pad, stride=8)
            parts.append(own[rows, :] + other[rows, :])
        x = jnp.concatenate(parts, axis=1)
        gram = gram + dot3(x, x, NT_DIMS)
    ri = lax.broadcasted_iota(jnp.int32, (pad, pad), 0)
    ci = lax.broadcasted_iota(jnp.int32, (pad, pad), 1)
    diagonal = jnp.where(ri == ci, gram, 0.0)
    dcol = jnp.sum(diagonal, axis=1, keepdims=True)
    drow = jnp.sum(diagonal, axis=0, keepdims=True)
    icol = 1.0 / jnp.sqrt(dcol * (1.0 / TESTS) + 1e-06)
    irow = 1.0 / jnp.sqrt(drow * (1.0 / TESTS) + 1e-06)
    norm = (gram * (icol * (1.0 / TESTS))) * irow
    norm = jnp.where(ci < TERMS, norm, 0.0)
    corr = norm[:TERMS, :TERMS]
    squares = jnp.sum(jnp.sum(corr * corr, axis=0, keepdims=True), axis=1, keepdims=True)
    normal[...] = norm[:, :TERMS]
    gi = lax.broadcasted_iota(jnp.int32, (GROUPS, TERMS), 0)
    onehot = gi == grp[...]
    products = [0.0] * (HALF + 2)
    for s in range(2):
        right = norm[TERMS + s : TERMS + s + 1, :TERMS]
        d = dot3(jnp.where(onehot, right, 0.0), corr, NN_DIMS)
        dmat[pl.ds(s * GROUPS, GROUPS), :] = d
        products[0] = products[0] + d * d
        for shift in range(1, HALF):
            products[shift] = products[shift] + d * jnp.concatenate([d[shift:], d[:shift]], axis=0)
        products[HALF] = products[HALF] + d * right
        products[HALF + 1] = products[HALF + 1] + right * right
    used = HALF * GROUPS + GROUPS + 1
    products[HALF + 1] = jnp.concatenate(
        [products[HALF + 1], jnp.zeros((WIDTH - used, TERMS), f32)], axis=0
    )
    high, low = split(jnp.concatenate(products, axis=0))
    members = onehot.astype(f32).astype(bf16)
    sums = dot(members, high, NT_DIMS) + dot(members, low, NT_DIMS)
    col = lax.broadcasted_iota(jnp.int32, (GROUPS, WIDTH), 1)
    payload[...] = jnp.where(col == WIDTH - 1, squares, sums)


def fit(own, other, grp):
    vmem = pl.BlockSpec(memory_space=pltpu.VMEM)
    return pl.pallas_call(
        fit_kernel,
        out_shape=(
            jax.ShapeDtypeStruct((GROUPS, WIDTH), f32),
            jax.ShapeDtypeStruct((TERMS + 8, TERMS), f32),
            jax.ShapeDtypeStruct((2 * GROUPS, TERMS), f32),
        ),
        in_specs=[vmem] * 3,
        out_specs=(vmem,) * 3,
        compiler_params=pltpu.CompilerParams(vmem_limit_bytes=VMEM_LIMIT),
        name="fit",
    )(own, other, grp)


def end_kernel(shares, grp, normal, dmat, *refs):
    pieces = refs[:shares]
    coef, misfit = refs[shares:]
    total = pieces[0][...]
    largest = total[:1, WIDTH - 1 :]
    for piece in pieces[1:]:
        value = piece[...]
        total = total + value
        largest = jnp.maximum(largest, value[:1, WIDTH - 1 :])
    step = 1.0 / jnp.sqrt(largest)
    first = HALF * GROUPS

    def factor(totals):
        threshold = 0.7 * jnp.sqrt(jnp.sum(totals, axis=0, keepdims=True) * (1.0 / GROUPS))
        return jnp.maximum(0.0, 1.0 - threshold / jnp.sqrt(totals + 1e-12))

    squares = total[:, first + GROUPS : first + GROUPS + 1]
    f_col = factor(step * step * squares)
    col = lax.broadcasted_iota(jnp.int32, (GROUPS, WIDTH), 1)
    group = lax.broadcasted_iota(jnp.int32, (GROUPS, WIDTH), 0)
    shift = jnp.zeros((GROUPS, WIDTH), jnp.int32)
    for k in range(1, HALF + 1):
        shift = jnp.where(col >= k * GROUPS, k, shift)
    one = col - shift * GROUPS
    two = one + shift
    two = jnp.where(two >= GROUPS, two - GROUPS, two)
    f_one = jnp.sum(jnp.where(group == one, f_col, 0.0), axis=0, keepdims=True)
    f_two = jnp.sum(jnp.where(group == two, f_col, 0.0), axis=0, keepdims=True)
    col, shift = col[:1], shift[:1]
    twice = jnp.where((shift == 0) | (shift == HALF - 1), 1.0, 2.0)
    pairs = jnp.where(col < first, twice * f_one * f_two, 0.0)
    singles = jnp.where((col >= first) & (col < first + GROUPS), f_one, 0.0)
    quad = jnp.sum(total * pairs, axis=1, keepdims=True)
    cross = jnp.sum(total * singles, axis=1, keepdims=True)
    grow = 1.0 + f_col
    totals = grow * grow * squares - 2.0 * step * grow * cross + step * step * quad
    f2_col = factor(jnp.maximum(step * step * totals, 0.0))
    term_group = lax.broadcasted_iota(jnp.int32, (GROUPS, TERMS), 0)
    onehot = term_group == grp[...]
    f_term = jnp.sum(jnp.where(onehot, f_col, 0.0), axis=0, keepdims=True)
    f2_term = jnp.sum(jnp.where(onehot, f2_col, 0.0), axis=0, keepdims=True)
    seconds = []
    for s in range(2):
        right = normal[pl.ds(TERMS + s, 1), :]
        pulled = jnp.sum(dmat[pl.ds(s * GROUPS, GROUPS), :] * f_col, axis=0, keepdims=True)
        seconds.append(step * ((1.0 + f_term) * right - step * pulled) * f2_term)
    second = jnp.concatenate(seconds + [jnp.zeros((6, TERMS), f32)], axis=0)
    coef[0] = (second / step)[:2]
    moved = dot3(second, normal[pl.ds(0, TERMS), :], NN_DIMS)
    misfit[0] = normal[pl.ds(TERMS, 2), :] - moved[:2]


def end(grp, normal, dmat, pieces):
    vmem = pl.BlockSpec(memory_space=pltpu.VMEM)
    shape = jax.ShapeDtypeStruct((1, 2, TERMS), f32)
    return pl.pallas_call(
        functools.partial(end_kernel, len(pieces)),
        out_shape=(shape, shape),
        in_specs=[vmem] * (3 + len(pieces)),
        out_specs=(vmem, vmem),
        compiler_params=pltpu.CompilerParams(vmem_limit_bytes=VMEM_LIMIT),
        name="finish",
    )(grp, normal, dmat, *pieces)


def partner(index, k, size):
    return index ^ k if size & (size - 1) == 0 else (index + k) % size


def neighbour_last(size):
    return (*range(2, size), 1) if size > 1 else ()


def exchange(value, axis, k):
    size = lax.axis_size(axis)
    return lax.ppermute(value, axis, [(partner(i, k, size), i) for i in range(size)])


def body(fields, library, centers_x, centers_y, centers_t, groups):
    pgroup = fields.shape[0]
    shares = lax.axis_size("term")
    local = library.shape[0]
    library = library.T
    if pgroup != shares or local * shares != TERMS or shares & (shares - 1):
        raise ValueError("unexpected split")
    libs = [library] + [exchange(library, "term", k) for k in range(1, shares)]
    flat = integrals(centers_x, centers_y, centers_t, fields)
    own = pick(libs, flat)
    spaces = lax.axis_size("space")
    others = [exchange(own, "space", k) for k in range(1, spaces)]
    grp = groups.reshape(1, TERMS)
    payload, normal, dmat = fit(own, sum(others[1:], others[0]), grp)
    col = lax.broadcasted_iota(jnp.int32, payload.shape, 1)
    params = lax.axis_size("param")
    pieces = [payload]
    for k in neighbour_last(shares):
        pieces.append(exchange(payload, "term", k))
    total = sum(pieces[1:], pieces[0])
    largest = functools.reduce(jnp.maximum, pieces)
    payload = jnp.where(col == WIDTH - 1, largest, total)
    pieces = [payload]
    for k in neighbour_last(params):
        pieces.append(exchange(payload, "param", k))
    return end(grp, normal, dmat, pieces)


def solution(mesh):
    return jax.shard_map(
        body,
        mesh=mesh,
        in_specs=(P("param", None, None, "space", None), P("term", None), P(), P(), P(), P()),
        out_specs=(P(("param", "term"), None, None), P(("param", "term"), None, None)),
        check_vma=False,
    )
```

```python
import functools

import jax
import jax.numpy as jnp
from jax import lax
from jax.experimental import pallas as pl
from jax.experimental.pallas import tpu as pltpu
from jax.sharding import PartitionSpec as P

NX = 128
NY = 128
NT = 8
POWERS = 7
TERMS = 168
TESTS = 1024
KX = 16
KY = 16
KT = 4
RX = 16
RT = 4
GROUPS = 24
ROWS = 3 * KY
LANES = 4 * KT * KX
HALF = GROUPS // 2 + 1
WIDTH = 384
VMEM_LIMIT = 40 * 2**20

f32, bf16 = jnp.float32, jnp.bfloat16
NT_DIMS = ((1,), (1,))
NN_DIMS = ((1,), (0,))


def split(x):
    high = x.astype(bf16)
    return high, (x - high.astype(f32)).astype(bf16)


def dot(a, b, dims):
    return lax.dot_general(a, b, (dims, ((), ())), preferred_element_type=f32)


def dot3(a, b, dims):
    ah, al = split(a)
    bh, bl = split(b)
    return dot(ah, bh, dims) + (dot(ah, bl, dims) + dot(al, bh, dims))


def space_rows(offset):
    scaled = offset.astype(f32) * (1.0 / RX)
    base = 1.0 - scaled * scaled
    inside = jnp.abs(scaled) < 1.0
    cube = base * base * base
    value = jnp.where(inside, cube * base, 0.0)
    first = jnp.where(inside, 8.0 * scaled * cube * (1.0 / RX), 0.0)
    second = jnp.where(
        inside, -8.0 * (cube - 6.0 * scaled * scaled * base * base) * (1.0 / (RX * RX)), 0.0
    )
    return value, first, second


def integrals_kernel(
    rows, centers_x, centers_y, centers_t, fields, out,
    cx, cy, ct, pair, u_cells, power_u, powers_v, y_split, tx_split, high, low, sem,
):
    cells = NT * rows
    first_row = lax.axis_index("space") * rows
    copy = pltpu.make_async_copy(fields.at[lax.axis_index("term")], pair, sem.at[0])
    small = [
        pltpu.make_async_copy(source, target, sem.at[1 + i])
        for i, (source, target) in enumerate(((centers_x, cx), (centers_y, cy), (centers_t, ct)))
    ]
    for one in small:
        one.start()
    copy.start()
    for one in small:
        one.wait()
    row = lax.broadcasted_iota(jnp.int32, (KY, NY), 0)
    lane = lax.broadcasted_iota(jnp.int32, (KY, NY), 1)
    center = jnp.zeros((KY, NY), jnp.int32)
    for k in range(KY):
        center = jnp.where(row == k, cy[k], center)
    offset = ((lane - center + NY // 2) & (NY - 1)) - NY // 2
    for i, part in enumerate(split(jnp.concatenate(space_rows(offset), axis=0))):
        y_split[pl.ds(i * ROWS, ROWS), :] = jnp.concatenate([part, part], axis=1)
    lane = lax.broadcasted_iota(jnp.int32, (1, LANES), 1)
    slot, kt, kx = lane >> 6, (lane >> 4) & 3, lane & 15
    center_x = jnp.zeros((1, LANES), jnp.int32)
    center_t = jnp.zeros((1, LANES), jnp.int32)
    for k in range(KX):
        center_x = jnp.where(kx == k, cx[k], center_x)
    for k in range(KT):
        center_t = jnp.where(kt == k, ct[k], center_t)
    row = lax.broadcasted_iota(jnp.int32, (rows, LANES), 0) + first_row
    offset = ((row - center_x + NX // 2) & (NX - 1)) - NX // 2
    value, first, second = space_rows(offset)
    x_table = jnp.where(slot == 1, first, jnp.where(slot == 2, second, value))
    for t in range(NT):
        scaled = (t - center_t).astype(f32) * (1.0 / RT)
        base = 1.0 - scaled * scaled
        weight = jnp.where(slot == 3, 4.0 * scaled * base * (1.0 / RT), base * base)
        weight = jnp.where(jnp.abs(scaled) < 1.0, weight, 0.0)
        for i, part in enumerate(split(x_table * weight)):
            tx_split[i, pl.ds(t * rows, rows), :] = part
    copy.wait()
    u = pair[0].reshape(cells, NY).T
    v = pair[1].reshape(cells, NY).T
    power_u[...] = u
    u_cells[...] = u
    power = v
    powers_v[0] = v
    for b in range(1, POWERS - 1):
        power = power * v
        powers_v[b] = power
    tile = 256
    span = POWERS * ROWS

    def contract(a):
        result = (
            dot(high[a & 1], tx_split[0], NN_DIMS)
            + dot(low[a & 1], tx_split[0], NN_DIMS)
            + dot(high[a & 1], tx_split[1], NN_DIMS)
        )
        out[0, pl.ds(a * span, span), :] = result[:, :128]
        out[1, pl.ds(a * span, span), :] = result[:, 128:]

    for a in range(POWERS):
        if a > 1:
            power_u[...] = power_u[...] * u_cells[...]
        for b in range(POWERS):
            for h in range(cells // tile):
                part = pl.ds(h * tile, tile)
                factors = ([power_u[:, part]] if a else []) + ([powers_v[b - 1, :, part]] if b else [])
                monomial = factors[0] if factors else jnp.ones((NY, tile), f32)
                if len(factors) > 1:
                    monomial = monomial * factors[1]
                both = jnp.concatenate(split(monomial), axis=0)
                across = dot(y_split[...], both, NN_DIMS)
                across_high, across_low = split(across[:ROWS] + across[ROWS:])
                high[a & 1, pl.ds( b * ROWS, ROWS), part] = across_high
                low[a & 1, pl.ds( b * ROWS, ROWS), part] = across_low
        if a: contract(a - 1)
    contract(POWERS - 1)


def integrals(cx, cy, ct, fields):
    rows = fields.shape[3]
    cells = NT * rows
    operands = [pltpu.with_memory_space_constraint(x, pltpu.HBM) for x in (cx, cy, ct, fields)]
    return pl.pallas_call(
        functools.partial(integrals_kernel, rows),
        out_shape=jax.ShapeDtypeStruct((2, POWERS * POWERS * ROWS, 128), f32),
        in_specs=[pl.BlockSpec(memory_space=pltpu.HBM)] * 4,
        out_specs=pl.BlockSpec(memory_space=pltpu.VMEM),
        scratch_shapes=[
            pltpu.SMEM((KX,), jnp.int32),
            pltpu.SMEM((KY,), jnp.int32),
            pltpu.SMEM((KT,), jnp.int32),
            pltpu.VMEM((2, NT, rows, NY), f32),
            pltpu.VMEM((NY, cells), f32),
            pltpu.VMEM((NY, cells), f32),
            pltpu.VMEM((POWERS - 1, NY, cells), f32),
            pltpu.VMEM((2 * ROWS, 2 * NY), bf16),
            pltpu.VMEM((2, cells, LANES), bf16),
            pltpu.VMEM((2, POWERS * ROWS, cells), bf16),
            pltpu.VMEM((2, POWERS * ROWS, cells), bf16),
            pltpu.SemaphoreType.DMA((4,)),
        ],
        compiler_params=pltpu.CompilerParams(vmem_limit_bytes=VMEM_LIMIT),
        cost_estimate=pl.CostEstimate(flops=10**10, bytes_accessed=3 * 10**6, transcendentals=0),
        name="integrals",
    )(*operands)


def pick_kernel(local, *refs):
    *libs, flat, out = refs
    left = lax.broadcasted_iota(jnp.int32, (8, 128), 1) < 64
    me = lax.axis_index("term")

    def load(a, b, dx, dy):
        row = pl.multiple_of((a * POWERS + b) * ROWS + dy * KY, 8)
        chunk = dx >> 1
        return (dx & 1) == 1, flat[chunk, pl.ds(row, 8), :], flat[chunk, pl.ds(row + 8, 8), :]

    def store(j, odd, top, low):
        even_value = jnp.where(left, top, pltpu.roll(low, 64, 1))
        odd_value = jnp.where(left, pltpu.roll(top, 64, 1), low)
        out[pl.ds(pl.multiple_of(j * 8, 8), 8), :] = jnp.where(odd, odd_value, even_value)

    done = 0
    for lib in libs:
        for k in range(lib.shape[0] // 4):
            first = (me ^ done) * local
            loaded = [load(*(lib[4 * k + part, n] for part in range(4))) for n in range(local)]
            for n in range(local):
                store(first + n, *loaded[n])
            done += 1
    store(TERMS, *load(1, 0, 3, 0))
    store(TERMS + 1, *load(0, 1, 3, 0))
    out[pl.ds((TERMS + 2) * 8, 48), :] = jnp.zeros((48, 128), f32)


def pick(libs, flat):
    smem = pl.BlockSpec(memory_space=pltpu.SMEM)
    vmem = pl.BlockSpec(memory_space=pltpu.VMEM)
    return pl.pallas_call(
        functools.partial(pick_kernel, libs[0].shape[1]),
        out_shape=jax.ShapeDtypeStruct(((TERMS + 8) * 8, 128), f32),
        in_specs=[smem] * len(libs) + [vmem],
        out_specs=vmem,
        compiler_params=pltpu.CompilerParams(vmem_limit_bytes=VMEM_LIMIT),
        name="pick",
    )(*libs, flat)


def fit_kernel(own, other, grp, payload, normal, dmat):
    pad = TERMS + 8
    gram = jnp.zeros((pad, pad), f32)
    for q in range(4):
        parts = []
        for s in (2 * q, 2 * q + 1):
            rows = pl.ds(s, pad, stride=8)
            parts.append(own[rows, :] + other[rows, :])
        x = jnp.concatenate(parts, axis=1)
        gram = gram + dot3(x, x, NT_DIMS)
    ri = lax.broadcasted_iota(jnp.int32, (pad, pad), 0)
    ci = lax.broadcasted_iota(jnp.int32, (pad, pad), 1)
    diagonal = jnp.where(ri == ci, gram, 0.0)
    dcol = jnp.sum(diagonal, axis=1, keepdims=True)
    drow = jnp.sum(diagonal, axis=0, keepdims=True)
    icol = 1.0 / jnp.sqrt(dcol * (1.0 / TESTS) + 1e-06)
    irow = 1.0 / jnp.sqrt(drow * (1.0 / TESTS) + 1e-06)
    norm = (gram * (icol * (1.0 / TESTS))) * irow
    norm = jnp.where(ci < TERMS, norm, 0.0)
    corr = norm[:TERMS, :TERMS]
    squares = jnp.sum(jnp.sum(corr * corr, axis=0, keepdims=True), axis=1, keepdims=True)
    normal[...] = norm[:, :TERMS]
    gi = lax.broadcasted_iota(jnp.int32, (GROUPS, TERMS), 0)
    onehot = gi == grp[...]
    products = [0.0] * (HALF + 2)
    for s in range(2):
        right = norm[TERMS + s : TERMS + s + 1, :TERMS]
        d = dot3(jnp.where(onehot, right, 0.0), corr, NN_DIMS)
        dmat[pl.ds(s * GROUPS, GROUPS), :] = d
        products[0] = products[0] + d * d
        for shift in range(1, HALF):
            products[shift] = products[shift] + d * jnp.concatenate([d[shift:], d[:shift]], axis=0)
        products[HALF] = products[HALF] + d * right
        products[HALF + 1] = products[HALF + 1] + right * right
    used = HALF * GROUPS + GROUPS + 1
    products[HALF + 1] = jnp.concatenate(
        [products[HALF + 1], jnp.zeros((WIDTH - used, TERMS), f32)], axis=0
    )
    high, low = split(jnp.concatenate(products, axis=0))
    members = onehot.astype(f32).astype(bf16)
    sums = dot(members, high, NT_DIMS) + dot(members, low, NT_DIMS)
    col = lax.broadcasted_iota(jnp.int32, (GROUPS, WIDTH), 1)
    payload[...] = jnp.where(col == WIDTH - 1, squares, sums)


def fit(own, other, grp):
    vmem = pl.BlockSpec(memory_space=pltpu.VMEM)
    return pl.pallas_call(
        fit_kernel,
        out_shape=(
            jax.ShapeDtypeStruct((GROUPS, WIDTH), f32),
            jax.ShapeDtypeStruct((TERMS + 8, TERMS), f32),
            jax.ShapeDtypeStruct((2 * GROUPS, TERMS), f32),
        ),
        in_specs=[vmem] * 3,
        out_specs=(vmem,) * 3,
        compiler_params=pltpu.CompilerParams(vmem_limit_bytes=VMEM_LIMIT),
        name="fit",
    )(own, other, grp)


def end_kernel(shares, grp, normal, dmat, *refs):
    pieces = refs[:shares]
    coef, misfit = refs[shares:]
    total = pieces[0][...]
    largest = total[:1, WIDTH - 1 :]
    for piece in pieces[1:]:
        value = piece[...]
        total = total + value
        largest = jnp.maximum(largest, value[:1, WIDTH - 1 :])
    step = 1.0 / jnp.sqrt(largest)
    first = HALF * GROUPS

    def factor(totals):
        threshold = 0.7 * jnp.sqrt(jnp.sum(totals, axis=0, keepdims=True) * (1.0 / GROUPS))
        return jnp.maximum(0.0, 1.0 - threshold / jnp.sqrt(totals + 1e-12))

    squares = total[:, first + GROUPS : first + GROUPS + 1]
    f_col = factor(step * step * squares)
    col = lax.broadcasted_iota(jnp.int32, (GROUPS, WIDTH), 1)
    group = lax.broadcasted_iota(jnp.int32, (GROUPS, WIDTH), 0)
    shift = jnp.zeros((GROUPS, WIDTH), jnp.int32)
    for k in range(1, HALF + 1):
        shift = jnp.where(col >= k * GROUPS, k, shift)
    one = col - shift * GROUPS
    two = one + shift
    two = jnp.where(two >= GROUPS, two - GROUPS, two)
    f_one = jnp.sum(jnp.where(group == one, f_col, 0.0), axis=0, keepdims=True)
    f_two = jnp.sum(jnp.where(group == two, f_col, 0.0), axis=0, keepdims=True)
    col, shift = col[:1], shift[:1]
    twice = jnp.where((shift == 0) | (shift == HALF - 1), 1.0, 2.0)
    pairs = jnp.where(col < first, twice * f_one * f_two, 0.0)
    singles = jnp.where((col >= first) & (col < first + GROUPS), f_one, 0.0)
    quad = jnp.sum(total * pairs, axis=1, keepdims=True)
    cross = jnp.sum(total * singles, axis=1, keepdims=True)
    grow = 1.0 + f_col
    totals = grow * grow * squares - 2.0 * step * grow * cross + step * step * quad
    f2_col = factor(jnp.maximum(step * step * totals, 0.0))
    term_group = lax.broadcasted_iota(jnp.int32, (GROUPS, TERMS), 0)
    onehot = term_group == grp[...]
    f_term = jnp.sum(jnp.where(onehot, f_col, 0.0), axis=0, keepdims=True)
    f2_term = jnp.sum(jnp.where(onehot, f2_col, 0.0), axis=0, keepdims=True)
    seconds = []
    for s in range(2):
        right = normal[pl.ds(TERMS + s, 1), :]
        pulled = jnp.sum(dmat[pl.ds(s * GROUPS, GROUPS), :] * f_col, axis=0, keepdims=True)
        seconds.append(step * ((1.0 + f_term) * right - step * pulled) * f2_term)
    second = jnp.concatenate(seconds + [jnp.zeros((6, TERMS), f32)], axis=0)
    coef[0] = (second / step)[:2]
    moved = dot3(second, normal[pl.ds(0, TERMS), :], NN_DIMS)
    misfit[0] = normal[pl.ds(TERMS, 2), :] - moved[:2]


def end(grp, normal, dmat, pieces):
    vmem = pl.BlockSpec(memory_space=pltpu.VMEM)
    shape = jax.ShapeDtypeStruct((1, 2, TERMS), f32)
    return pl.pallas_call(
        functools.partial(end_kernel, len(pieces)),
        out_shape=(shape, shape),
        in_specs=[vmem] * (3 + len(pieces)),
        out_specs=(vmem, vmem),
        compiler_params=pltpu.CompilerParams(vmem_limit_bytes=VMEM_LIMIT),
        name="finish",
    )(grp, normal, dmat, *pieces)


def partner(index, k, size):
    return index ^ k if size & (size - 1) == 0 else (index + k) % size


def neighbour_last(size):
    return (*range(2, size), 1) if size > 1 else ()


def exchange(value, axis, k):
    size = lax.axis_size(axis)
    return lax.ppermute(value, axis, [(partner(i, k, size), i) for i in range(size)])


def shared_exchange(value, axis):
    size = lax.axis_size(axis)
    rounds = []
    for first in range(0, size, 2):
        steps = [(core, first + 2 - core) for core in range(2) if first + 2 - core < size]
        pairs = [
            (core * size + partner(i, k, size), core * size + i)
            for core, k in steps
            for i in range(size)
        ]
        rounds.append(lax.ppermute(value, ("space", axis), pairs))
    return rounds


def merge(values, own_core=None):
    col = lax.broadcasted_iota(jnp.int32, values[0].shape, 1)
    largest = functools.reduce(jnp.maximum, values)
    if own_core is not None:
        values = [jnp.where(lax.axis_index("space") == own_core, values[0], 0.0)] + values[1:]
    return jnp.where(col == WIDTH - 1, largest, sum(values[1:], values[0]))


def body(fields, library, centers_x, centers_y, centers_t, groups):
    pgroup = fields.shape[0]
    shares = lax.axis_size("term")
    local = library.shape[0]
    library = library.T
    spaces = lax.axis_size("space")
    if spaces != 2 or pgroup != shares or local * shares != TERMS or shares & (shares - 1):
        raise ValueError("unexpected split")
    libs = [library] + [exchange(library, "term", k) for k in range(1, shares)]
    flat = integrals(centers_x, centers_y, centers_t, fields)
    own = pick(libs, flat)
    grp = groups.reshape(1, TERMS)
    payload, normal, dmat = fit(own, exchange(own, "space", 1), grp)
    params = lax.axis_size("param")
    payload = merge([payload] + shared_exchange(payload, "term"), 0)
    payload = merge([payload] + [exchange(payload, "param", k) for k in neighbour_last(params)])
    return end(grp, normal, dmat, [payload, exchange(payload, "space", 1)])


def solution(mesh):
    return jax.shard_map(
        body,
        mesh=mesh,
        in_specs=(P("param", None, None, "space", None), P("term", None), P(), P(), P(), P()),
        out_specs=(P(("param", "term"), None, None), P(("param", "term"), None, None)),
        check_vma=False,
    )
```

```python
import functools

import jax
import jax.numpy as jnp
from jax import lax
from jax.experimental import pallas as pl
from jax.experimental.pallas import tpu as pltpu
from jax.sharding import PartitionSpec as P

NX = 128
NY = 128
NT = 8
POWERS = 7
TERMS = 168
TESTS = 1024
KX = 16
KY = 16
KT = 4
RX = 16
RT = 4
GROUPS = 24
ROWS = 3 * KY
LANES = 4 * KT * KX
HALF = GROUPS // 2 + 1
WIDTH = 384
VMEM_LIMIT = 40 * 2**20

f32, bf16 = jnp.float32, jnp.bfloat16
NT_DIMS = ((1,), (1,))
NN_DIMS = ((1,), (0,))


def split(x):
    high = x.astype(bf16)
    return high, (x - high.astype(f32)).astype(bf16)


def dot(a, b, dims):
    return lax.dot_general(a, b, (dims, ((), ())), preferred_element_type=f32)


def dot3(a, b, dims):
    ah, al = split(a)
    bh, bl = split(b)
    return dot(ah, bh, dims) + (dot(ah, bl, dims) + dot(al, bh, dims))


def space_rows(offset):
    scaled = offset.astype(f32) * (1.0 / RX)
    base = 1.0 - scaled * scaled
    inside = jnp.abs(scaled) < 1.0
    cube = base * base * base
    value = jnp.where(inside, cube * base, 0.0)
    first = jnp.where(inside, 8.0 * scaled * cube * (1.0 / RX), 0.0)
    second = jnp.where(
        inside, -8.0 * (cube - 6.0 * scaled * scaled * base * base) * (1.0 / (RX * RX)), 0.0
    )
    return value, first, second


def integrals_kernel(
    rows, centers_x, centers_y, centers_t, fields, out,
    cx, cy, ct, pair, u_cells, power_u, powers_v, y_split, tx_split, high, low, sem,
):
    cells = NT * rows
    first_row = lax.axis_index("space") * rows
    copy = pltpu.make_async_copy(fields.at[lax.axis_index("term")], pair, sem.at[0])
    small = [
        pltpu.make_async_copy(source, target, sem.at[1 + i])
        for i, (source, target) in enumerate(((centers_x, cx), (centers_y, cy), (centers_t, ct)))
    ]
    for one in small:
        one.start()
    copy.start()
    for one in small:
        one.wait()
    row = lax.broadcasted_iota(jnp.int32, (KY, NY), 0)
    lane = lax.broadcasted_iota(jnp.int32, (KY, NY), 1)
    center = jnp.zeros((KY, NY), jnp.int32)
    for k in range(KY):
        center = jnp.where(row == k, cy[k], center)
    offset = ((lane - center + NY // 2) & (NY - 1)) - NY // 2
    rest = jnp.concatenate(space_rows(offset), axis=0)
    for i in range(3):
        part = rest.astype(bf16)
        rest = rest - part.astype(f32)
        y_split[pl.ds(i * ROWS, ROWS), :] = jnp.concatenate([part, part], axis=1)
    lane = lax.broadcasted_iota(jnp.int32, (1, LANES), 1)
    slot, kt, kx = lane >> 6, (lane >> 4) & 3, lane & 15
    center_x = jnp.zeros((1, LANES), jnp.int32)
    center_t = jnp.zeros((1, LANES), jnp.int32)
    for k in range(KX):
        center_x = jnp.where(kx == k, cx[k], center_x)
    for k in range(KT):
        center_t = jnp.where(kt == k, ct[k], center_t)
    row = lax.broadcasted_iota(jnp.int32, (rows, LANES), 0) + first_row
    offset = ((row - center_x + NX // 2) & (NX - 1)) - NX // 2
    value, first, second = space_rows(offset)
    x_table = jnp.where(slot == 1, first, jnp.where(slot == 2, second, value))
    for t in range(NT):
        scaled = (t - center_t).astype(f32) * (1.0 / RT)
        base = 1.0 - scaled * scaled
        weight = jnp.where(slot == 3, 4.0 * scaled * base * (1.0 / RT), base * base)
        weight = jnp.where(jnp.abs(scaled) < 1.0, weight, 0.0)
        for i, part in enumerate(split(x_table * weight)):
            tx_split[i, pl.ds(t * rows, rows), :] = part
    copy.wait()
    u = pair[0].reshape(cells, NY).T
    v = pair[1].reshape(cells, NY).T
    power_u[...] = u
    u_cells[...] = u
    power = v
    powers_v[0] = v
    for b in range(1, POWERS - 1):
        power = power * v
        powers_v[b] = power
    tile = 256
    span = POWERS * ROWS

    def contract(a):
        result = (
            dot(high[a & 1], tx_split[0], NN_DIMS)
            + dot(low[a & 1], tx_split[0], NN_DIMS)
            + dot(high[a & 1], tx_split[1], NN_DIMS)
        )
        out[0, pl.ds(a * span, span), :] = result[:, :128]
        out[1, pl.ds(a * span, span), :] = result[:, 128:]

    for a in range(POWERS):
        if a > 1:
            power_u[...] = power_u[...] * u_cells[...]
        for b in range(POWERS):
            for h in range(cells // tile):
                part = pl.ds(h * tile, tile)
                factors = ([power_u[:, part]] if a else []) + ([powers_v[b - 1, :, part]] if b else [])
                monomial = factors[0] if factors else jnp.ones((NY, tile), f32)
                if len(factors) > 1:
                    monomial = monomial * factors[1]
                both = jnp.concatenate(split(monomial), axis=0)
                across = dot(y_split[...], both, NN_DIMS)
                across_high, across_low = split(
                    across[:ROWS] + (across[ROWS : 2 * ROWS] + across[2 * ROWS :])
                )
                high[a & 1, pl.ds( b * ROWS, ROWS), part] = across_high
                low[a & 1, pl.ds( b * ROWS, ROWS), part] = across_low
        if a: contract(a - 1)
    contract(POWERS - 1)


def integrals(cx, cy, ct, fields):
    rows = fields.shape[3]
    cells = NT * rows
    operands = [pltpu.with_memory_space_constraint(x, pltpu.HBM) for x in (cx, cy, ct, fields)]
    return pl.pallas_call(
        functools.partial(integrals_kernel, rows),
        out_shape=jax.ShapeDtypeStruct((2, POWERS * POWERS * ROWS, 128), f32),
        in_specs=[pl.BlockSpec(memory_space=pltpu.HBM)] * 4,
        out_specs=pl.BlockSpec(memory_space=pltpu.VMEM),
        scratch_shapes=[
            pltpu.SMEM((KX,), jnp.int32),
            pltpu.SMEM((KY,), jnp.int32),
            pltpu.SMEM((KT,), jnp.int32),
            pltpu.VMEM((2, NT, rows, NY), f32),
            pltpu.VMEM((NY, cells), f32),
            pltpu.VMEM((NY, cells), f32),
            pltpu.VMEM((POWERS - 1, NY, cells), f32),
            pltpu.VMEM((3 * ROWS, 2 * NY), bf16),
            pltpu.VMEM((2, cells, LANES), bf16),
            pltpu.VMEM((2, POWERS * ROWS, cells), bf16),
            pltpu.VMEM((2, POWERS * ROWS, cells), bf16),
            pltpu.SemaphoreType.DMA((4,)),
        ],
        compiler_params=pltpu.CompilerParams(vmem_limit_bytes=VMEM_LIMIT),
        cost_estimate=pl.CostEstimate(flops=10**10, bytes_accessed=3 * 10**6, transcendentals=0),
        name="integrals",
    )(*operands)


def pick_kernel(local, *refs):
    *libs, flat, out = refs
    left = lax.broadcasted_iota(jnp.int32, (8, 128), 1) < 64
    me = lax.axis_index("term")

    def load(a, b, dx, dy):
        row = pl.multiple_of((a * POWERS + b) * ROWS + dy * KY, 8)
        chunk = dx >> 1
        return (dx & 1) == 1, flat[chunk, pl.ds(row, 8), :], flat[chunk, pl.ds(row + 8, 8), :]

    def store(j, odd, top, low):
        even_value = jnp.where(left, top, pltpu.roll(low, 64, 1))
        odd_value = jnp.where(left, pltpu.roll(top, 64, 1), low)
        out[pl.ds(pl.multiple_of(j * 8, 8), 8), :] = jnp.where(odd, odd_value, even_value)

    done = 0
    for lib in libs:
        for k in range(lib.shape[0] // 4):
            first = (me ^ done) * local
            loaded = [load(*(lib[4 * k + part, n] for part in range(4))) for n in range(local)]
            for n in range(local):
                store(first + n, *loaded[n])
            done += 1
    store(TERMS, *load(1, 0, 3, 0))
    store(TERMS + 1, *load(0, 1, 3, 0))
    out[pl.ds((TERMS + 2) * 8, 48), :] = jnp.zeros((48, 128), f32)


def pick(libs, flat):
    smem = pl.BlockSpec(memory_space=pltpu.SMEM)
    vmem = pl.BlockSpec(memory_space=pltpu.VMEM)
    return pl.pallas_call(
        functools.partial(pick_kernel, libs[0].shape[1]),
        out_shape=jax.ShapeDtypeStruct(((TERMS + 8) * 8, 128), f32),
        in_specs=[smem] * len(libs) + [vmem],
        out_specs=vmem,
        compiler_params=pltpu.CompilerParams(vmem_limit_bytes=VMEM_LIMIT),
        name="pick",
    )(*libs, flat)


def fit_kernel(own, other, grp, payload, normal, dmat):
    pad = TERMS + 8
    gram = jnp.zeros((pad, pad), f32)
    for q in range(4):
        parts = []
        for s in (2 * q, 2 * q + 1):
            rows = pl.ds(s, pad, stride=8)
            parts.append(own[rows, :] + other[rows, :])
        x = jnp.concatenate(parts, axis=1)
        gram = gram + dot3(x, x, NT_DIMS)
    ri = lax.broadcasted_iota(jnp.int32, (pad, pad), 0)
    ci = lax.broadcasted_iota(jnp.int32, (pad, pad), 1)
    diagonal = jnp.where(ri == ci, gram, 0.0)
    dcol = jnp.sum(diagonal, axis=1, keepdims=True)
    drow = jnp.sum(diagonal, axis=0, keepdims=True)
    icol = 1.0 / jnp.sqrt(dcol * (1.0 / TESTS) + 1e-06)
    irow = 1.0 / jnp.sqrt(drow * (1.0 / TESTS) + 1e-06)
    norm = (gram * (icol * (1.0 / TESTS))) * irow
    norm = jnp.where(ci < TERMS, norm, 0.0)
    corr = norm[:TERMS, :TERMS]
    squares = jnp.sum(jnp.sum(corr * corr, axis=0, keepdims=True), axis=1, keepdims=True)
    normal[...] = norm[:, :TERMS]
    gi = lax.broadcasted_iota(jnp.int32, (GROUPS, TERMS), 0)
    onehot = gi == grp[...]
    products = [0.0] * (HALF + 2)
    for s in range(2):
        right = norm[TERMS + s : TERMS + s + 1, :TERMS]
        d = dot3(jnp.where(onehot, right, 0.0), corr, NN_DIMS)
        dmat[pl.ds(s * GROUPS, GROUPS), :] = d
        products[0] = products[0] + d * d
        for shift in range(1, HALF):
            products[shift] = products[shift] + d * jnp.concatenate([d[shift:], d[:shift]], axis=0)
        products[HALF] = products[HALF] + d * right
        products[HALF + 1] = products[HALF + 1] + right * right
    used = HALF * GROUPS + GROUPS + 1
    products[HALF + 1] = jnp.concatenate(
        [products[HALF + 1], jnp.zeros((WIDTH - used, TERMS), f32)], axis=0
    )
    high, low = split(jnp.concatenate(products, axis=0))
    members = onehot.astype(f32).astype(bf16)
    sums = dot(members, high, NT_DIMS) + dot(members, low, NT_DIMS)
    col = lax.broadcasted_iota(jnp.int32, (GROUPS, WIDTH), 1)
    payload[...] = jnp.where(col == WIDTH - 1, squares, sums)


def fit(own, other, grp):
    vmem = pl.BlockSpec(memory_space=pltpu.VMEM)
    return pl.pallas_call(
        fit_kernel,
        out_shape=(
            jax.ShapeDtypeStruct((GROUPS, WIDTH), f32),
            jax.ShapeDtypeStruct((TERMS + 8, TERMS), f32),
            jax.ShapeDtypeStruct((2 * GROUPS, TERMS), f32),
        ),
        in_specs=[vmem] * 3,
        out_specs=(vmem,) * 3,
        compiler_params=pltpu.CompilerParams(vmem_limit_bytes=VMEM_LIMIT),
        name="fit",
    )(own, other, grp)


def end_kernel(shares, grp, normal, dmat, *refs):
    pieces = refs[:shares]
    coef, misfit = refs[shares:]
    total = pieces[0][...]
    largest = total[:1, WIDTH - 1 :]
    for piece in pieces[1:]:
        value = piece[...]
        total = total + value
        largest = jnp.maximum(largest, value[:1, WIDTH - 1 :])
    step = 1.0 / jnp.sqrt(largest)
    first = HALF * GROUPS

    def factor(totals):
        threshold = 0.7 * jnp.sqrt(jnp.sum(totals, axis=0, keepdims=True) * (1.0 / GROUPS))
        return jnp.maximum(0.0, 1.0 - threshold / jnp.sqrt(totals + 1e-12))

    squares = total[:, first + GROUPS : first + GROUPS + 1]
    f_col = factor(step * step * squares)
    col = lax.broadcasted_iota(jnp.int32, (GROUPS, WIDTH), 1)
    group = lax.broadcasted_iota(jnp.int32, (GROUPS, WIDTH), 0)
    shift = jnp.zeros((GROUPS, WIDTH), jnp.int32)
    for k in range(1, HALF + 1):
        shift = jnp.where(col >= k * GROUPS, k, shift)
    one = col - shift * GROUPS
    two = one + shift
    two = jnp.where(two >= GROUPS, two - GROUPS, two)
    f_one = jnp.sum(jnp.where(group == one, f_col, 0.0), axis=0, keepdims=True)
    f_two = jnp.sum(jnp.where(group == two, f_col, 0.0), axis=0, keepdims=True)
    col, shift = col[:1], shift[:1]
    twice = jnp.where((shift == 0) | (shift == HALF - 1), 1.0, 2.0)
    pairs = jnp.where(col < first, twice * f_one * f_two, 0.0)
    singles = jnp.where((col >= first) & (col < first + GROUPS), f_one, 0.0)
    quad = jnp.sum(total * pairs, axis=1, keepdims=True)
    cross = jnp.sum(total * singles, axis=1, keepdims=True)
    grow = 1.0 + f_col
    totals = grow * grow * squares - 2.0 * step * grow * cross + step * step * quad
    f2_col = factor(jnp.maximum(step * step * totals, 0.0))
    term_group = lax.broadcasted_iota(jnp.int32, (GROUPS, TERMS), 0)
    onehot = term_group == grp[...]
    f_term = jnp.sum(jnp.where(onehot, f_col, 0.0), axis=0, keepdims=True)
    f2_term = jnp.sum(jnp.where(onehot, f2_col, 0.0), axis=0, keepdims=True)
    seconds = []
    for s in range(2):
        right = normal[pl.ds(TERMS + s, 1), :]
        pulled = jnp.sum(dmat[pl.ds(s * GROUPS, GROUPS), :] * f_col, axis=0, keepdims=True)
        seconds.append(step * ((1.0 + f_term) * right - step * pulled) * f2_term)
    second = jnp.concatenate(seconds + [jnp.zeros((6, TERMS), f32)], axis=0)
    coef[0] = (second / step)[:2]
    moved = dot3(second, normal[pl.ds(0, TERMS), :], NN_DIMS)
    misfit[0] = normal[pl.ds(TERMS, 2), :] - moved[:2]


def end(grp, normal, dmat, pieces):
    vmem = pl.BlockSpec(memory_space=pltpu.VMEM)
    shape = jax.ShapeDtypeStruct((1, 2, TERMS), f32)
    return pl.pallas_call(
        functools.partial(end_kernel, len(pieces)),
        out_shape=(shape, shape),
        in_specs=[vmem] * (3 + len(pieces)),
        out_specs=(vmem, vmem),
        compiler_params=pltpu.CompilerParams(vmem_limit_bytes=VMEM_LIMIT),
        name="finish",
    )(grp, normal, dmat, *pieces)


def partner(index, k, size):
    return index ^ k if size & (size - 1) == 0 else (index + k) % size


def neighbour_last(size):
    return (*range(2, size), 1) if size > 1 else ()


def exchange(value, axis, k):
    size = lax.axis_size(axis)
    return lax.ppermute(value, axis, [(partner(i, k, size), i) for i in range(size)])


def shared_exchange(value, axis):
    size = lax.axis_size(axis)
    rounds = []
    for first in range(0, size, 2):
        steps = [(core, first + 2 - core) for core in range(2) if first + 2 - core < size]
        pairs = [
            (core * size + partner(i, k, size), core * size + i)
            for core, k in steps
            for i in range(size)
        ]
        rounds.append(lax.ppermute(value, ("space", axis), pairs))
    return rounds


def merge(values, own_core=None):
    col = lax.broadcasted_iota(jnp.int32, values[0].shape, 1)
    largest = functools.reduce(jnp.maximum, values)
    if own_core is not None:
        values = [jnp.where(lax.axis_index("space") == own_core, values[0], 0.0)] + values[1:]
    return jnp.where(col == WIDTH - 1, largest, sum(values[1:], values[0]))


def body(fields, library, centers_x, centers_y, centers_t, groups):
    pgroup = fields.shape[0]
    shares = lax.axis_size("term")
    local = library.shape[0]
    library = library.T
    spaces = lax.axis_size("space")
    if spaces != 2 or pgroup != shares or local * shares != TERMS or shares & (shares - 1):
        raise ValueError("unexpected split")
    libs = [library] + [exchange(library, "term", k) for k in range(1, shares)]
    flat = integrals(centers_x, centers_y, centers_t, fields)
    own = pick(libs, flat)
    grp = groups.reshape(1, TERMS)
    payload, normal, dmat = fit(own, exchange(own, "space", 1), grp)
    params = lax.axis_size("param")
    payload = merge([payload] + shared_exchange(payload, "term"), 0)
    payload = merge([payload] + [exchange(payload, "param", k) for k in neighbour_last(params)])
    return end(grp, normal, dmat, [payload, exchange(payload, "space", 1)])


def solution(mesh):
    return jax.shard_map(
        body,
        mesh=mesh,
        in_specs=(P("param", None, None, "space", None), P("term", None), P(), P(), P(), P()),
        out_specs=(P(("param", "term"), None, None), P(("param", "term"), None, None)),
        check_vma=False,
    )
```

```python
import functools

import jax
import jax.numpy as jnp
from jax import lax
from jax.experimental import pallas as pl
from jax.experimental.pallas import tpu as pltpu
from jax.sharding import PartitionSpec as P

NX = 128
NY = 128
NT = 8
POWERS = 7
TERMS = 168
TESTS = 1024
KX = 16
KY = 16
KT = 4
RX = 16
RT = 4
GROUPS = 24
ROWS = 3 * KY
LANES = 4 * KT * KX
HALF = GROUPS // 2 + 1
WIDTH = 384
VMEM_LIMIT = 40 * 2**20

f32, bf16 = jnp.float32, jnp.bfloat16
NT_DIMS = ((1,), (1,))
NN_DIMS = ((1,), (0,))


def split(x):
    high = x.astype(bf16)
    return high, (x - high.astype(f32)).astype(bf16)


def dot(a, b, dims):
    return lax.dot_general(a, b, (dims, ((), ())), preferred_element_type=f32)


def dot3(a, b, dims):
    ah, al = split(a)
    bh, bl = split(b)
    return dot(ah, bh, dims) + (dot(ah, bl, dims) + dot(al, bh, dims))


def space_rows(offset):
    scaled = offset.astype(f32) * (1.0 / RX)
    base = 1.0 - scaled * scaled
    inside = jnp.abs(scaled) < 1.0
    cube = base * base * base
    value = jnp.where(inside, cube * base, 0.0)
    first = jnp.where(inside, 8.0 * scaled * cube * (1.0 / RX), 0.0)
    second = jnp.where(
        inside, -8.0 * (cube - 6.0 * scaled * scaled * base * base) * (1.0 / (RX * RX)), 0.0
    )
    return value, first, second


def integrals_kernel(
    rows, centers_x, centers_y, centers_t, fields, out,
    cx, cy, ct, pair, u_cells, power_u, powers_v, y_split, tx_split, high, low, sem,
):
    cells = NT * rows
    first_row = lax.axis_index("space") * rows
    copy = pltpu.make_async_copy(fields.at[lax.axis_index("term")], pair, sem.at[0])
    small = [
        pltpu.make_async_copy(source, target, sem.at[1 + i])
        for i, (source, target) in enumerate(((centers_x, cx), (centers_y, cy), (centers_t, ct)))
    ]
    for one in small:
        one.start()
    copy.start()
    for one in small:
        one.wait()
    row = lax.broadcasted_iota(jnp.int32, (KY, NY), 0)
    lane = lax.broadcasted_iota(jnp.int32, (KY, NY), 1)
    center = jnp.zeros((KY, NY), jnp.int32)
    for k in range(KY):
        center = jnp.where(row == k, cy[k], center)
    offset = ((lane - center + NY // 2) & (NY - 1)) - NY // 2
    rest = jnp.concatenate(space_rows(offset), axis=0)
    for i in range(3):
        part = rest.astype(bf16)
        rest = rest - part.astype(f32)
        y_split[pl.ds(i * ROWS, ROWS), :] = jnp.concatenate([part, part], axis=1)
    lane = lax.broadcasted_iota(jnp.int32, (1, LANES), 1)
    slot, kt, kx = lane >> 6, (lane >> 4) & 3, lane & 15
    center_x = jnp.zeros((1, LANES), jnp.int32)
    center_t = jnp.zeros((1, LANES), jnp.int32)
    for k in range(KX):
        center_x = jnp.where(kx == k, cx[k], center_x)
    for k in range(KT):
        center_t = jnp.where(kt == k, ct[k], center_t)
    row = lax.broadcasted_iota(jnp.int32, (rows, LANES), 0) + first_row
    offset = ((row - center_x + NX // 2) & (NX - 1)) - NX // 2
    value, first, second = space_rows(offset)
    x_table = jnp.where(slot == 1, first, jnp.where(slot == 2, second, value))
    for t in range(NT):
        scaled = (t - center_t).astype(f32) * (1.0 / RT)
        base = 1.0 - scaled * scaled
        weight = jnp.where(slot == 3, 4.0 * scaled * base * (1.0 / RT), base * base)
        weight = jnp.where(jnp.abs(scaled) < 1.0, weight, 0.0)
        for i, part in enumerate(split(x_table * weight)):
            tx_split[i, pl.ds(t * rows, rows), :] = part
    copy.wait()
    u = pair[0].reshape(cells, NY).T
    v = pair[1].reshape(cells, NY).T
    power_u[...] = u
    u_cells[...] = u
    power = v
    powers_v[0] = v
    for b in range(1, POWERS - 1):
        power = power * v
        powers_v[b] = power
    tile = 256
    span = POWERS * ROWS

    def contract(a):
        result = (
            dot(high[a & 1], tx_split[0], NN_DIMS)
            + dot(low[a & 1], tx_split[0], NN_DIMS)
            + dot(high[a & 1], tx_split[1], NN_DIMS)
        )
        out[0, pl.ds(a * span, span), :] = result[:, :128]
        out[1, pl.ds(a * span, span), :] = result[:, 128:]

    for a in range(POWERS):
        if a > 1:
            power_u[...] = power_u[...] * u_cells[...]
        for b in range(POWERS):
            for h in range(cells // tile):
                part = pl.ds(h * tile, tile)
                factors = ([power_u[:, part]] if a else []) + ([powers_v[b - 1, :, part]] if b else [])
                monomial = factors[0] if factors else jnp.ones((NY, tile), f32)
                if len(factors) > 1:
                    monomial = monomial * factors[1]
                both = jnp.concatenate(split(monomial), axis=0)
                across = dot(y_split[...], both, NN_DIMS)
                across_high, across_low = split(
                    across[:ROWS] + (across[ROWS : 2 * ROWS] + across[2 * ROWS :])
                )
                high[a & 1, pl.ds( b * ROWS, ROWS), part] = across_high
                low[a & 1, pl.ds( b * ROWS, ROWS), part] = across_low
        if a: contract(a - 1)
    contract(POWERS - 1)


def integrals(cx, cy, ct, fields):
    rows = fields.shape[3]
    cells = NT * rows
    operands = [pltpu.with_memory_space_constraint(x, pltpu.HBM) for x in (cx, cy, ct, fields)]
    return pl.pallas_call(
        functools.partial(integrals_kernel, rows),
        out_shape=jax.ShapeDtypeStruct((2, POWERS * POWERS * ROWS, 128), f32),
        in_specs=[pl.BlockSpec(memory_space=pltpu.HBM)] * 4,
        out_specs=pl.BlockSpec(memory_space=pltpu.VMEM),
        scratch_shapes=[
            pltpu.SMEM((KX,), jnp.int32),
            pltpu.SMEM((KY,), jnp.int32),
            pltpu.SMEM((KT,), jnp.int32),
            pltpu.VMEM((2, NT, rows, NY), f32),
            pltpu.VMEM((NY, cells), f32),
            pltpu.VMEM((NY, cells), f32),
            pltpu.VMEM((POWERS - 1, NY, cells), f32),
            pltpu.VMEM((3 * ROWS, 2 * NY), bf16),
            pltpu.VMEM((2, cells, LANES), bf16),
            pltpu.VMEM((2, POWERS * ROWS, cells), bf16),
            pltpu.VMEM((2, POWERS * ROWS, cells), bf16),
            pltpu.SemaphoreType.DMA((4,)),
        ],
        compiler_params=pltpu.CompilerParams(vmem_limit_bytes=VMEM_LIMIT),
        cost_estimate=pl.CostEstimate(flops=10**10, bytes_accessed=3 * 10**6, transcendentals=0),
        name="integrals",
    )(*operands)


def pick_kernel(local, *refs):
    *libs, flat, out = refs
    left = lax.broadcasted_iota(jnp.int32, (8, 128), 1) < 64
    me = lax.axis_index("term")

    def load(a, b, dx, dy):
        row = pl.multiple_of((a * POWERS + b) * ROWS + dy * KY, 8)
        chunk = dx >> 1
        return (dx & 1) == 1, flat[chunk, pl.ds(row, 8), :], flat[chunk, pl.ds(row + 8, 8), :]

    def store(j, odd, top, low):
        even_value = jnp.where(left, top, pltpu.roll(low, 64, 1))
        odd_value = jnp.where(left, pltpu.roll(top, 64, 1), low)
        out[pl.ds(pl.multiple_of(j * 8, 8), 8), :] = jnp.where(odd, odd_value, even_value)

    done = 0
    for lib in libs:
        for k in range(lib.shape[0] // 4):
            first = (me ^ done) * local
            loaded = [load(*(lib[4 * k + part, n] for part in range(4))) for n in range(local)]
            for n in range(local):
                store(first + n, *loaded[n])
            done += 1
    store(TERMS, *load(1, 0, 3, 0))
    store(TERMS + 1, *load(0, 1, 3, 0))
    out[pl.ds((TERMS + 2) * 8, 48), :] = jnp.zeros((48, 128), f32)


def pick(libs, flat):
    smem = pl.BlockSpec(memory_space=pltpu.SMEM)
    vmem = pl.BlockSpec(memory_space=pltpu.VMEM)
    return pl.pallas_call(
        functools.partial(pick_kernel, libs[0].shape[1]),
        out_shape=jax.ShapeDtypeStruct(((TERMS + 8) * 8, 128), f32),
        in_specs=[smem] * len(libs) + [vmem],
        out_specs=vmem,
        compiler_params=pltpu.CompilerParams(vmem_limit_bytes=VMEM_LIMIT),
        name="pick",
    )(*libs, flat)


def fit_kernel(own, other, grp, payload, normal, dmat):
    pad = TERMS + 8
    gram = jnp.zeros((pad, pad), f32)
    cross = jnp.zeros((pad, pad), f32)
    for q in range(4):
        parts = []
        for s in (2 * q, 2 * q + 1):
            rows = pl.ds(s, pad, stride=8)
            parts.append(own[rows, :] + other[rows, :])
        high, low = split(jnp.concatenate(parts, axis=1))
        gram = gram + dot(high, high, NT_DIMS)
        cross = cross + dot(high, low, NT_DIMS)
    gram = gram + (cross + cross.T)
    ri = lax.broadcasted_iota(jnp.int32, (pad, pad), 0)
    ci = lax.broadcasted_iota(jnp.int32, (pad, pad), 1)
    diagonal = jnp.where(ri == ci, gram, 0.0)
    dcol = jnp.sum(diagonal, axis=1, keepdims=True)
    drow = jnp.sum(diagonal, axis=0, keepdims=True)
    icol = 1.0 / jnp.sqrt(dcol * (1.0 / TESTS) + 1e-06)
    irow = 1.0 / jnp.sqrt(drow * (1.0 / TESTS) + 1e-06)
    norm = (gram * (icol * (1.0 / TESTS))) * irow
    norm = jnp.where(ci < TERMS, norm, 0.0)
    corr = norm[:TERMS, :TERMS]
    squares = jnp.sum(jnp.sum(corr * corr, axis=0, keepdims=True), axis=1, keepdims=True)
    normal[...] = norm[:, :TERMS]
    gi = lax.broadcasted_iota(jnp.int32, (GROUPS, TERMS), 0)
    onehot = gi == grp[...]
    products = [0.0] * (HALF + 2)
    for s in range(2):
        right = norm[TERMS + s : TERMS + s + 1, :TERMS]
        d = dot3(jnp.where(onehot, right, 0.0), corr, NN_DIMS)
        dmat[pl.ds(s * GROUPS, GROUPS), :] = d
        products[0] = products[0] + d * d
        for shift in range(1, HALF):
            products[shift] = products[shift] + d * jnp.concatenate([d[shift:], d[:shift]], axis=0)
        products[HALF] = products[HALF] + d * right
        products[HALF + 1] = products[HALF + 1] + right * right
    used = HALF * GROUPS + GROUPS + 1
    products[HALF + 1] = jnp.concatenate(
        [products[HALF + 1], jnp.zeros((WIDTH - used, TERMS), f32)], axis=0
    )
    high, low = split(jnp.concatenate(products, axis=0))
    members = onehot.astype(f32).astype(bf16)
    sums = dot(members, high, NT_DIMS) + dot(members, low, NT_DIMS)
    col = lax.broadcasted_iota(jnp.int32, (GROUPS, WIDTH), 1)
    payload[...] = jnp.where(col == WIDTH - 1, squares, sums)


def fit(own, other, grp):
    vmem = pl.BlockSpec(memory_space=pltpu.VMEM)
    return pl.pallas_call(
        fit_kernel,
        out_shape=(
            jax.ShapeDtypeStruct((GROUPS, WIDTH), f32),
            jax.ShapeDtypeStruct((TERMS + 8, TERMS), f32),
            jax.ShapeDtypeStruct((2 * GROUPS, TERMS), f32),
        ),
        in_specs=[vmem] * 3,
        out_specs=(vmem,) * 3,
        compiler_params=pltpu.CompilerParams(vmem_limit_bytes=VMEM_LIMIT),
        name="fit",
    )(own, other, grp)


def end_kernel(shares, grp, normal, dmat, *refs):
    pieces = refs[:shares]
    coef, misfit = refs[shares:]
    total = pieces[0][...]
    largest = total[:1, WIDTH - 1 :]
    for piece in pieces[1:]:
        value = piece[...]
        total = total + value
        largest = jnp.maximum(largest, value[:1, WIDTH - 1 :])
    step = 1.0 / jnp.sqrt(largest)
    first = HALF * GROUPS

    def factor(totals):
        threshold = 0.7 * jnp.sqrt(jnp.sum(totals, axis=0, keepdims=True) * (1.0 / GROUPS))
        return jnp.maximum(0.0, 1.0 - threshold / jnp.sqrt(totals + 1e-12))

    squares = total[:, first + GROUPS : first + GROUPS + 1]
    f_col = factor(step * step * squares)
    col = lax.broadcasted_iota(jnp.int32, (GROUPS, WIDTH), 1)
    group = lax.broadcasted_iota(jnp.int32, (GROUPS, WIDTH), 0)
    shift = jnp.zeros((GROUPS, WIDTH), jnp.int32)
    for k in range(1, HALF + 1):
        shift = jnp.where(col >= k * GROUPS, k, shift)
    one = col - shift * GROUPS
    two = one + shift
    two = jnp.where(two >= GROUPS, two - GROUPS, two)
    f_one = jnp.sum(jnp.where(group == one, f_col, 0.0), axis=0, keepdims=True)
    f_two = jnp.sum(jnp.where(group == two, f_col, 0.0), axis=0, keepdims=True)
    col, shift = col[:1], shift[:1]
    twice = jnp.where((shift == 0) | (shift == HALF - 1), 1.0, 2.0)
    pairs = jnp.where(col < first, twice * f_one * f_two, 0.0)
    singles = jnp.where((col >= first) & (col < first + GROUPS), f_one, 0.0)
    quad = jnp.sum(total * pairs, axis=1, keepdims=True)
    cross = jnp.sum(total * singles, axis=1, keepdims=True)
    grow = 1.0 + f_col
    totals = grow * grow * squares - 2.0 * step * grow * cross + step * step * quad
    f2_col = factor(jnp.maximum(step * step * totals, 0.0))
    term_group = lax.broadcasted_iota(jnp.int32, (GROUPS, TERMS), 0)
    onehot = term_group == grp[...]
    f_term = jnp.sum(jnp.where(onehot, f_col, 0.0), axis=0, keepdims=True)
    f2_term = jnp.sum(jnp.where(onehot, f2_col, 0.0), axis=0, keepdims=True)
    seconds = []
    for s in range(2):
        right = normal[pl.ds(TERMS + s, 1), :]
        pulled = jnp.sum(dmat[pl.ds(s * GROUPS, GROUPS), :] * f_col, axis=0, keepdims=True)
        seconds.append(step * ((1.0 + f_term) * right - step * pulled) * f2_term)
    second = jnp.concatenate(seconds + [jnp.zeros((6, TERMS), f32)], axis=0)
    coef[0] = (second / step)[:2]
    moved = dot3(second, normal[pl.ds(0, TERMS), :], NN_DIMS)
    misfit[0] = normal[pl.ds(TERMS, 2), :] - moved[:2]


def end(grp, normal, dmat, pieces):
    vmem = pl.BlockSpec(memory_space=pltpu.VMEM)
    shape = jax.ShapeDtypeStruct((1, 2, TERMS), f32)
    return pl.pallas_call(
        functools.partial(end_kernel, len(pieces)),
        out_shape=(shape, shape),
        in_specs=[vmem] * (3 + len(pieces)),
        out_specs=(vmem, vmem),
        compiler_params=pltpu.CompilerParams(vmem_limit_bytes=VMEM_LIMIT),
        name="finish",
    )(grp, normal, dmat, *pieces)


def partner(index, k, size):
    return index ^ k if size & (size - 1) == 0 else (index + k) % size


def neighbour_last(size):
    return (*range(2, size), 1) if size > 1 else ()


def exchange(value, axis, k):
    size = lax.axis_size(axis)
    return lax.ppermute(value, axis, [(partner(i, k, size), i) for i in range(size)])


def shared_exchange(value, axis):
    size = lax.axis_size(axis)
    rounds = []
    for first in range(0, size, 2):
        steps = [(core, first + 2 - core) for core in range(2) if first + 2 - core < size]
        pairs = [
            (core * size + partner(i, k, size), core * size + i)
            for core, k in steps
            for i in range(size)
        ]
        rounds.append(lax.ppermute(value, ("space", axis), pairs))
    return rounds


def merge(values, own_core=None):
    col = lax.broadcasted_iota(jnp.int32, values[0].shape, 1)
    largest = functools.reduce(jnp.maximum, values)
    if own_core is not None:
        values = [jnp.where(lax.axis_index("space") == own_core, values[0], 0.0)] + values[1:]
    return jnp.where(col == WIDTH - 1, largest, sum(values[1:], values[0]))


def body(fields, library, centers_x, centers_y, centers_t, groups):
    pgroup = fields.shape[0]
    shares = lax.axis_size("term")
    local = library.shape[0]
    library = library.T
    spaces = lax.axis_size("space")
    if spaces != 2 or pgroup != shares or local * shares != TERMS or shares & (shares - 1):
        raise ValueError("unexpected split")
    libs = [library] + [exchange(library, "term", k) for k in range(1, shares)]
    flat = integrals(centers_x, centers_y, centers_t, fields)
    own = pick(libs, flat)
    grp = groups.reshape(1, TERMS)
    payload, normal, dmat = fit(own, exchange(own, "space", 1), grp)
    params = lax.axis_size("param")
    payload = merge([payload] + shared_exchange(payload, "term"), 0)
    payload = merge([payload] + [exchange(payload, "param", k) for k in neighbour_last(params)])
    return end(grp, normal, dmat, [payload, exchange(payload, "space", 1)])


def solution(mesh):
    return jax.shard_map(
        body,
        mesh=mesh,
        in_specs=(P("param", None, None, "space", None), P("term", None), P(), P(), P(), P()),
        out_specs=(P(("param", "term"), None, None), P(("param", "term"), None, None)),
        check_vma=False,
    )
```

```python
import functools

import jax
import jax.numpy as jnp
from jax import lax
from jax.experimental import pallas as pl
from jax.experimental.pallas import tpu as pltpu
from jax.sharding import PartitionSpec as P

NX = 128
NY = 128
NT = 8
POWERS = 7
TERMS = 168
TESTS = 1024
KX = 16
KY = 16
KT = 4
RX = 16
RT = 4
GROUPS = 24
ROWS = 3 * KY
LANES = 4 * KT * KX
HALF = GROUPS // 2 + 1
WIDTH = 384
VMEM_LIMIT = 40 * 2**20

f32, bf16 = jnp.float32, jnp.bfloat16
NT_DIMS = ((1,), (1,))
NN_DIMS = ((1,), (0,))


def split(x):
    high = x.astype(bf16)
    return high, (x - high.astype(f32)).astype(bf16)


def dot(a, b, dims):
    return lax.dot_general(a, b, (dims, ((), ())), preferred_element_type=f32)


def dot3(a, b, dims):
    ah, al = split(a)
    bh, bl = split(b)
    return dot(ah, bh, dims) + (dot(ah, bl, dims) + dot(al, bh, dims))


def space_rows(offset):
    scaled = offset.astype(f32) * (1.0 / RX)
    base = 1.0 - scaled * scaled
    inside = jnp.abs(scaled) < 1.0
    cube = base * base * base
    value = jnp.where(inside, cube * base, 0.0)
    first = jnp.where(inside, 8.0 * scaled * cube * (1.0 / RX), 0.0)
    second = jnp.where(
        inside, -8.0 * (cube - 6.0 * scaled * scaled * base * base) * (1.0 / (RX * RX)), 0.0
    )
    return value, first, second


def integrals_kernel(
    rows, centers_x, centers_y, centers_t, fields, out,
    cx, cy, ct, pair, u_cells, power_u, powers_v, y_split, tx_split, high, low, sem,
):
    cells = NT * rows
    first_row = lax.axis_index("space") * rows
    copy = pltpu.make_async_copy(fields.at[lax.axis_index("term")], pair, sem.at[0])
    small = [
        pltpu.make_async_copy(source, target, sem.at[1 + i])
        for i, (source, target) in enumerate(((centers_x, cx), (centers_y, cy), (centers_t, ct)))
    ]
    for one in small:
        one.start()
    copy.start()
    for one in small:
        one.wait()
    row = lax.broadcasted_iota(jnp.int32, (KY, NY), 0)
    lane = lax.broadcasted_iota(jnp.int32, (KY, NY), 1)
    center = jnp.zeros((KY, NY), jnp.int32)
    for k in range(KY):
        center = jnp.where(row == k, cy[k], center)
    offset = ((lane - center + NY // 2) & (NY - 1)) - NY // 2
    rest = jnp.concatenate(space_rows(offset), axis=0)
    for i in range(3):
        part = rest.astype(bf16)
        rest = rest - part.astype(f32)
        y_split[pl.ds(i * ROWS, ROWS), :] = jnp.concatenate([part, part], axis=1)
    lane = lax.broadcasted_iota(jnp.int32, (1, LANES), 1)
    slot, kt, kx = lane >> 6, (lane >> 4) & 3, lane & 15
    center_x = jnp.zeros((1, LANES), jnp.int32)
    center_t = jnp.zeros((1, LANES), jnp.int32)
    for k in range(KX):
        center_x = jnp.where(kx == k, cx[k], center_x)
    for k in range(KT):
        center_t = jnp.where(kt == k, ct[k], center_t)
    row = lax.broadcasted_iota(jnp.int32, (rows, LANES), 0) + first_row
    offset = ((row - center_x + NX // 2) & (NX - 1)) - NX // 2
    value, first, second = space_rows(offset)
    x_table = jnp.where(slot == 1, first, jnp.where(slot == 2, second, value))
    for t in range(NT):
        scaled = (t - center_t).astype(f32) * (1.0 / RT)
        base = 1.0 - scaled * scaled
        weight = jnp.where(slot == 3, 4.0 * scaled * base * (1.0 / RT), base * base)
        weight = jnp.where(jnp.abs(scaled) < 1.0, weight, 0.0)
        for i, part in enumerate(split(x_table * weight)):
            tx_split[i, pl.ds(t * rows, rows), :] = part
    copy.wait()
    u = pair[0].reshape(cells, NY).T
    v = pair[1].reshape(cells, NY).T
    power_u[...] = u
    u_cells[...] = u
    power = v
    powers_v[0] = v
    for b in range(1, POWERS - 1):
        power = power * v
        powers_v[b] = power
    tile = 256
    span = POWERS * ROWS

    def contract(a):
        result = (
            dot(high[a & 1], tx_split[0], NN_DIMS)
            + dot(low[a & 1], tx_split[0], NN_DIMS)
            + dot(high[a & 1], tx_split[1], NN_DIMS)
        )
        out[0, pl.ds(a * span, span), :] = result[:, :128]
        out[1, pl.ds(a * span, span), :] = result[:, 128:]

    for a in range(POWERS):
        if a > 1:
            power_u[...] = power_u[...] * u_cells[...]
        for b in range(POWERS):
            for h in range(cells // tile):
                part = pl.ds(h * tile, tile)
                factors = ([power_u[:, part]] if a else []) + ([powers_v[b - 1, :, part]] if b else [])
                monomial = factors[0] if factors else jnp.ones((NY, tile), f32)
                if len(factors) > 1:
                    monomial = monomial * factors[1]
                both = jnp.concatenate(split(monomial), axis=0)
                across = dot(y_split[...], both, NN_DIMS)
                across_high, across_low = split(
                    across[:ROWS] + (across[ROWS : 2 * ROWS] + across[2 * ROWS :])
                )
                high[a & 1, pl.ds( b * ROWS, ROWS), part] = across_high
                low[a & 1, pl.ds( b * ROWS, ROWS), part] = across_low
        if a: contract(a - 1)
    contract(POWERS - 1)


def integrals(cx, cy, ct, fields):
    rows = fields.shape[3]
    cells = NT * rows
    operands = [pltpu.with_memory_space_constraint(x, pltpu.HBM) for x in (cx, cy, ct, fields)]
    return pl.pallas_call(
        functools.partial(integrals_kernel, rows),
        out_shape=jax.ShapeDtypeStruct((2, POWERS * POWERS * ROWS, 128), f32),
        in_specs=[pl.BlockSpec(memory_space=pltpu.HBM)] * 4,
        out_specs=pl.BlockSpec(memory_space=pltpu.VMEM),
        scratch_shapes=[
            pltpu.SMEM((KX,), jnp.int32),
            pltpu.SMEM((KY,), jnp.int32),
            pltpu.SMEM((KT,), jnp.int32),
            pltpu.VMEM((2, NT, rows, NY), f32),
            pltpu.VMEM((NY, cells), f32),
            pltpu.VMEM((NY, cells), f32),
            pltpu.VMEM((POWERS - 1, NY, cells), f32),
            pltpu.VMEM((3 * ROWS, 2 * NY), bf16),
            pltpu.VMEM((2, cells, LANES), bf16),
            pltpu.VMEM((2, POWERS * ROWS, cells), bf16),
            pltpu.VMEM((2, POWERS * ROWS, cells), bf16),
            pltpu.SemaphoreType.DMA((4,)),
        ],
        compiler_params=pltpu.CompilerParams(vmem_limit_bytes=VMEM_LIMIT),
        cost_estimate=pl.CostEstimate(flops=10**10, bytes_accessed=3 * 10**6, transcendentals=0),
        name="integrals",
    )(*operands)


def pick_kernel(local, *refs):
    *libs, flat, out = refs
    left = lax.broadcasted_iota(jnp.int32, (8, 128), 1) < 64
    me = lax.axis_index("term")

    def load(a, b, dx, dy):
        row = pl.multiple_of((a * POWERS + b) * ROWS + dy * KY, 8)
        chunk = dx >> 1
        return (dx & 1) == 1, flat[chunk, pl.ds(row, 8), :], flat[chunk, pl.ds(row + 8, 8), :]

    def store(j, odd, top, low):
        even_value = jnp.where(left, top, pltpu.roll(low, 64, 1))
        odd_value = jnp.where(left, pltpu.roll(top, 64, 1), low)
        out[pl.ds(pl.multiple_of(j * 8, 8), 8), :] = jnp.where(odd, odd_value, even_value)

    done = 0
    for lib in libs:
        for k in range(lib.shape[0] // 4):
            first = (me ^ done) * local
            loaded = [load(*(lib[4 * k + part, n] for part in range(4))) for n in range(local)]
            for n in range(local):
                store(first + n, *loaded[n])
            done += 1
    store(TERMS, *load(1, 0, 3, 0))
    store(TERMS + 1, *load(0, 1, 3, 0))
    out[pl.ds((TERMS + 2) * 8, 48), :] = jnp.zeros((48, 128), f32)


def pick(libs, flat):
    smem = pl.BlockSpec(memory_space=pltpu.SMEM)
    vmem = pl.BlockSpec(memory_space=pltpu.VMEM)
    return pl.pallas_call(
        functools.partial(pick_kernel, libs[0].shape[1]),
        out_shape=jax.ShapeDtypeStruct(((TERMS + 8) * 8, 128), f32),
        in_specs=[smem] * len(libs) + [vmem],
        out_specs=vmem,
        compiler_params=pltpu.CompilerParams(vmem_limit_bytes=VMEM_LIMIT),
        name="pick",
    )(*libs, flat)


def fit_kernel(own, other, grp, payload, normal, dmat):
    pad = TERMS + 8
    gram = jnp.zeros((pad, pad), f32)
    cross = jnp.zeros((pad, pad), f32)
    for q in range(4):
        parts = []
        for s in (2 * q, 2 * q + 1):
            rows = pl.ds(s, pad, stride=8)
            parts.append(own[rows, :] + other[rows, :])
        high, low = split(jnp.concatenate(parts, axis=1))
        gram = gram + dot(high, high, NT_DIMS)
        cross = cross + dot(high, low, NT_DIMS)
    gram = gram + (cross + cross.T)
    ri = lax.broadcasted_iota(jnp.int32, (pad, pad), 0)
    ci = lax.broadcasted_iota(jnp.int32, (pad, pad), 1)
    diagonal = jnp.where(ri == ci, gram, 0.0)
    dcol = jnp.sum(diagonal, axis=1, keepdims=True)
    drow = jnp.sum(diagonal, axis=0, keepdims=True)
    icol = 1.0 / jnp.sqrt(dcol * (1.0 / TESTS) + 1e-06)
    irow = 1.0 / jnp.sqrt(drow * (1.0 / TESTS) + 1e-06)
    norm = (gram * (icol * (1.0 / TESTS))) * irow
    norm = jnp.where(ci < TERMS, norm, 0.0)
    corr = norm[:TERMS, :TERMS]
    squares = jnp.sum(jnp.sum(corr * corr, axis=0, keepdims=True), axis=1, keepdims=True)
    normal[...] = norm[:, :TERMS]
    gi = lax.broadcasted_iota(jnp.int32, (GROUPS, TERMS), 0)
    onehot = gi == grp[...]
    spread = [jnp.where(onehot, norm[TERMS + s : TERMS + s + 1, :TERMS], 0.0) for s in range(2)]
    grouped = dot3(jnp.concatenate(spread, axis=0), corr, NN_DIMS)
    dmat[...] = grouped
    products = [0.0] * (HALF + 2)
    for s in range(2):
        right = norm[TERMS + s : TERMS + s + 1, :TERMS]
        d = grouped[s * GROUPS : (s + 1) * GROUPS]
        products[0] = products[0] + d * d
        for shift in range(1, HALF):
            products[shift] = products[shift] + d * jnp.concatenate([d[shift:], d[:shift]], axis=0)
        products[HALF] = products[HALF] + d * right
        products[HALF + 1] = products[HALF + 1] + right * right
    used = HALF * GROUPS + GROUPS + 1
    products[HALF + 1] = jnp.concatenate(
        [products[HALF + 1], jnp.zeros((WIDTH - used, TERMS), f32)], axis=0
    )
    high, low = split(jnp.concatenate(products, axis=0))
    members = onehot.astype(f32).astype(bf16)
    sums = dot(members, high, NT_DIMS) + dot(members, low, NT_DIMS)
    col = lax.broadcasted_iota(jnp.int32, (GROUPS, WIDTH), 1)
    payload[...] = jnp.where(col == WIDTH - 1, squares, sums)


def fit(own, other, grp):
    vmem = pl.BlockSpec(memory_space=pltpu.VMEM)
    return pl.pallas_call(
        fit_kernel,
        out_shape=(
            jax.ShapeDtypeStruct((GROUPS, WIDTH), f32),
            jax.ShapeDtypeStruct((TERMS + 8, TERMS), f32),
            jax.ShapeDtypeStruct((2 * GROUPS, TERMS), f32),
        ),
        in_specs=[vmem] * 3,
        out_specs=(vmem,) * 3,
        compiler_params=pltpu.CompilerParams(vmem_limit_bytes=VMEM_LIMIT),
        name="fit",
    )(own, other, grp)


def end_kernel(shares, grp, normal, dmat, *refs):
    pieces = refs[:shares]
    coef, misfit = refs[shares:]
    total = pieces[0][...]
    largest = total[:1, WIDTH - 1 :]
    for piece in pieces[1:]:
        value = piece[...]
        total = total + value
        largest = jnp.maximum(largest, value[:1, WIDTH - 1 :])
    step = 1.0 / jnp.sqrt(largest)
    first = HALF * GROUPS

    def factor(totals):
        threshold = 0.7 * jnp.sqrt(jnp.sum(totals, axis=0, keepdims=True) * (1.0 / GROUPS))
        return jnp.maximum(0.0, 1.0 - threshold / jnp.sqrt(totals + 1e-12))

    squares = total[:, first + GROUPS : first + GROUPS + 1]
    f_col = factor(step * step * squares)
    col = lax.broadcasted_iota(jnp.int32, (GROUPS, WIDTH), 1)
    group = lax.broadcasted_iota(jnp.int32, (GROUPS, WIDTH), 0)
    shift = jnp.zeros((GROUPS, WIDTH), jnp.int32)
    for k in range(1, HALF + 1):
        shift = jnp.where(col >= k * GROUPS, k, shift)
    one = col - shift * GROUPS
    two = one + shift
    two = jnp.where(two >= GROUPS, two - GROUPS, two)
    f_one = jnp.sum(jnp.where(group == one, f_col, 0.0), axis=0, keepdims=True)
    f_two = jnp.sum(jnp.where(group == two, f_col, 0.0), axis=0, keepdims=True)
    col, shift = col[:1], shift[:1]
    twice = jnp.where((shift == 0) | (shift == HALF - 1), 1.0, 2.0)
    pairs = jnp.where(col < first, twice * f_one * f_two, 0.0)
    singles = jnp.where((col >= first) & (col < first + GROUPS), f_one, 0.0)
    quad = jnp.sum(total * pairs, axis=1, keepdims=True)
    cross = jnp.sum(total * singles, axis=1, keepdims=True)
    grow = 1.0 + f_col
    totals = grow * grow * squares - 2.0 * step * grow * cross + step * step * quad
    f2_col = factor(jnp.maximum(step * step * totals, 0.0))
    term_group = lax.broadcasted_iota(jnp.int32, (GROUPS, TERMS), 0)
    onehot = term_group == grp[...]
    f_term = jnp.sum(jnp.where(onehot, f_col, 0.0), axis=0, keepdims=True)
    f2_term = jnp.sum(jnp.where(onehot, f2_col, 0.0), axis=0, keepdims=True)
    seconds = []
    for s in range(2):
        right = normal[pl.ds(TERMS + s, 1), :]
        pulled = jnp.sum(dmat[pl.ds(s * GROUPS, GROUPS), :] * f_col, axis=0, keepdims=True)
        seconds.append(step * ((1.0 + f_term) * right - step * pulled) * f2_term)
    second = jnp.concatenate(seconds + [jnp.zeros((6, TERMS), f32)], axis=0)
    coef[0] = (second / step)[:2]
    moved = dot3(second, normal[pl.ds(0, TERMS), :], NN_DIMS)
    misfit[0] = normal[pl.ds(TERMS, 2), :] - moved[:2]


def end(grp, normal, dmat, pieces):
    vmem = pl.BlockSpec(memory_space=pltpu.VMEM)
    shape = jax.ShapeDtypeStruct((1, 2, TERMS), f32)
    return pl.pallas_call(
        functools.partial(end_kernel, len(pieces)),
        out_shape=(shape, shape),
        in_specs=[vmem] * (3 + len(pieces)),
        out_specs=(vmem, vmem),
        compiler_params=pltpu.CompilerParams(vmem_limit_bytes=VMEM_LIMIT),
        name="finish",
    )(grp, normal, dmat, *pieces)


def partner(index, k, size):
    return index ^ k if size & (size - 1) == 0 else (index + k) % size


def neighbour_last(size):
    return (*range(2, size), 1) if size > 1 else ()


def exchange(value, axis, k):
    size = lax.axis_size(axis)
    return lax.ppermute(value, axis, [(partner(i, k, size), i) for i in range(size)])


def shared_exchange(value, axis):
    size = lax.axis_size(axis)
    rounds = []
    for first in range(0, size, 2):
        steps = [(core, first + 2 - core) for core in range(2) if first + 2 - core < size]
        pairs = [
            (core * size + partner(i, k, size), core * size + i)
            for core, k in steps
            for i in range(size)
        ]
        rounds.append(lax.ppermute(value, ("space", axis), pairs))
    return rounds


def merge(values, own_core=None):
    col = lax.broadcasted_iota(jnp.int32, values[0].shape, 1)
    largest = functools.reduce(jnp.maximum, values)
    if own_core is not None:
        values = [jnp.where(lax.axis_index("space") == own_core, values[0], 0.0)] + values[1:]
    return jnp.where(col == WIDTH - 1, largest, sum(values[1:], values[0]))


def body(fields, library, centers_x, centers_y, centers_t, groups):
    pgroup = fields.shape[0]
    shares = lax.axis_size("term")
    local = library.shape[0]
    library = library.T
    spaces = lax.axis_size("space")
    if spaces != 2 or pgroup != shares or local * shares != TERMS or shares & (shares - 1):
        raise ValueError("unexpected split")
    libs = [library] + [exchange(library, "term", k) for k in range(1, shares)]
    flat = integrals(centers_x, centers_y, centers_t, fields)
    own = pick(libs, flat)
    grp = groups.reshape(1, TERMS)
    payload, normal, dmat = fit(own, exchange(own, "space", 1), grp)
    params = lax.axis_size("param")
    payload = merge([payload] + shared_exchange(payload, "term"), 0)
    payload = merge([payload] + [exchange(payload, "param", k) for k in neighbour_last(params)])
    return end(grp, normal, dmat, [payload, exchange(payload, "space", 1)])


def solution(mesh):
    return jax.shard_map(
        body,
        mesh=mesh,
        in_specs=(P("param", None, None, "space", None), P("term", None), P(), P(), P(), P()),
        out_specs=(P(("param", "term"), None, None), P(("param", "term"), None, None)),
        check_vma=False,
    )
```
